32 devices in a mesh: dp: 8 (over z, x), shard: 4 (over y, core).
Axes of the slice: x: 2, y: 2, z: 4, core: 2. Of those that a mesh axis runs over, the one named last changes fastest.
Arguments:
- patches: bfloat16 [64, 1024, 384], P(('dp', 'shard')), may hold values from -6 to 6
- segments: int32 [64, 1024], P(('dp', 'shard')), may hold values from 0 to 7, never falling along the last dimension, each value on 1 to 256 neighbouring positions
- out_grad: bfloat16 [64, 1024, 384], P(('dp', 'shard')), may hold values from -6 to 6
- master: float32 [1775104], P('shard'), may hold values from -6 to 6
- moment_one: float32 [1775104], P('shard'), may hold values from -6 to 6
- moment_two: float32 [1775104], P('shard'), may hold values from 0.1 to 10
Outputs:
- activations: bfloat16 [64, 1024, 384], P(('dp', 'shard'))
- input_grad: bfloat16 [64, 1024, 384], P(('dp', 'shard'))
- grad_sum: float32 [1775104], P('shard')
- vector_grad: float32 [5632], replicated
- new_master: float32 [1775104], P('shard')
- new_moment_one: float32 [1775104], P('shard')
- new_moment_two: float32 [1775104], P('shard')
- weights_copy: bfloat16 [1775104], replicated
The draws below stay inside these ranges and needn't reach their ends.
All inputs are finite; a program needn't handle non-finite values.
Results may differ from the reference program's by a relative error of at most 0.015.
Values may be sent and summed in bfloat16 or wider, within the bound.
A program may use at most 192 MiB of HBM per device.

```python
import math
import jax
import jax.numpy as jnp
import numpy as np
from jax import lax

D = 384
HEADS = 6
HD = 64
FF = 1536
SEQ = 1024
STEP = 3
SEQS = 64
PARAMS = 1775104


def normal_piece(key, number, entry_count, spread):
    sub_key = jax.random.fold_in(key, number)
    return jax.random.truncated_normal(sub_key, -4.0, 4.0, (entry_count,), jnp.float32) * spread


def gain_piece(key, number, entry_count):
    sub_key = jax.random.fold_in(key, number)
    return jax.random.uniform(sub_key, (entry_count,), jnp.float32, 0.6, 1.4)


def draw_master(key, part):
    pieces = [normal_piece(key, 1, 3 * D * D, D ** (-0.5)), normal_piece(key, 2, D * D, 8.0 * D ** (-0.5)), normal_piece(key, 3, D * FF, D ** (-0.5)), normal_piece(key, 4, FF * D, FF ** (-0.5)), gain_piece(key, 5, D), normal_piece(key, 6, D, 0.2), normal_piece(key, 7, 3 * D, 0.2), gain_piece(key, 8, HD), normal_piece(key, 9, HD, 0.2), gain_piece(key, 10, HD), normal_piece(key, 11, HD, 0.2), normal_piece(key, 12, D, 0.2), gain_piece(key, 13, D), normal_piece(key, 14, D, 0.2), normal_piece(key, 15, FF, 0.2), normal_piece(key, 16, D, 0.2)]
    used_count = 4 * D * D + 2 * D * FF + 9 * D + FF + 4 * HD
    pieces.append(normal_piece(key, 17, PARAMS - used_count, 0.2))
    return jnp.concatenate(pieces)


def level_of(key, extent, shards, smallest, top_value):
    loudness, own = 1.0, jax.random.fold_in(key, 6)
    for axis_at, blocks in shards:
        heights = jnp.exp(jax.random.uniform(jax.random.fold_in(own, axis_at), (blocks,), jnp.float32, smallest / len(shards), top_value / len(shards)))
        loudness = loudness * jnp.repeat(heights, extent[axis_at] // blocks).reshape([-1 if axis == axis_at else 1 for axis in range(len(extent))])
    return loudness


def length_profile(count, total, most, lean):
    portions = [(1 << 20) // math.isqrt(grade ** lean) + 1 for grade in range(2, count + 1)]
    rest, given = total - most - (count - 1), [1] * (count - 1)
    while rest > 0:
        free = [i for i in range(count - 1) if given[i] < most]
        whole, remaining = sum([portions[i] for i in free]), rest
        for i in free:
            more = min(most - given[i], max(1, remaining * portions[i] // whole), rest)
            given[i] = given[i] + more
            rest = rest - more
    return np.array([most] + given)


def ragged(key, number_of, total, limit, slope):
    if number_of == 2:
        one = jax.random.randint(key, (), max(1, total - limit), min(limit, total - 1) + 1)
        return jnp.stack([one, total - one])
    sizes = jnp.asarray(length_profile(number_of, total, limit, slope), jnp.int32)
    couples = (number_of - 1) // 2
    donor, sink = sizes[1:1 + 2 * couples:2], sizes[2:2 + 2 * couples:2]
    margin = jnp.minimum(donor - 1, limit - sink)
    shifted = jax.random.randint(jax.random.fold_in(key, 1), (couples,), 0, 1 << 20) % (margin + 1)
    sizes = sizes.at[1:1 + 2 * couples:2].set(donor - shifted).at[2:2 + 2 * couples:2].set(sink + shifted)
    return sizes[jax.random.permutation(jax.random.fold_in(key, 2), number_of)]


def scatter_about(key, shape, deviation, limit, cuts=(), kind=jnp.bfloat16):
    entries = deviation * jax.random.normal(key, shape, jnp.float32)
    if cuts:
        entries = entries * level_of(key, shape, cuts, -0.22, 0.18)
    return jnp.clip(entries, -limit, limit).astype(kind)


def setup_inputs(seed: int = 0) -> dict:
    streams_of = jax.random.split(jax.random.key(seed), 7)
    return {
        "patches": scatter_about(streams_of[0], (SEQS, SEQ, D), 1.0, 6.0, ((0, 32),)),
        "segments": jax.vmap(lambda own: jnp.searchsorted(jnp.cumsum(ragged(own, max(SEQ // 128, 6), SEQ, SEQ // 4, 2)), jnp.arange(SEQ), side="right"))(jax.random.split(streams_of[1], SEQS)).reshape((SEQS, SEQ)).astype(jnp.int32),
        "out_grad": scatter_about(streams_of[2], (SEQS, SEQ, D), 1.0, 6.0, ((0, 32),)),
        "master": draw_master(jax.random.fold_in(streams_of[6], 71), 0),
        "moment_one": scatter_about(streams_of[4], (PARAMS,), 1.0, 6.0, ((0, 4),), jnp.float32),
        "moment_two": jnp.clip(jnp.exp(math.log(10.0) - 4.6051702 * jax.random.uniform(streams_of[5], (PARAMS,), jnp.float32) ** level_of(streams_of[5], (PARAMS,), ((0, 4),), -0.2, 0.2)), 0.1, 10.0),
    }


@jax.custom_vjp
def low(v):
    return lax.optimization_barrier(v.astype(jnp.bfloat16)).astype(jnp.float32)

@jax.custom_vjp
def low_back(v):
    return v

def low_keep(v):
    return (low(v), None)

def low_pass(kept, grad):
    return (grad,)

def back_keep(v):
    return (v, None)

def back_low(kept, grad):
    return (low(grad),)
low.defvjp(low_keep, low_pass)
low_back.defvjp(back_keep, back_low)
NORM_EPS = 1e-06
MASKED = -1e+30
BETA_ONE = 0.5
BETA_TWO = 0.5
RATE = 0.03
DECAY = 0.1
ADAM_EPS = 1e-08

def layout():
    return [('qkv_weight', (D, 3 * D)), ('out_weight', (D, D)), ('up_weight', (D, FF)), ('down_weight', (FF, D)), ('norm_gain', (D,)), ('norm_bias', (D,)), ('qkv_bias', (3 * D,)), ('query_gain', (HD,)), ('query_bias', (HD,)), ('key_gain', (HD,)), ('key_bias', (HD,)), ('out_bias', (D,)), ('mlp_gain', (D,)), ('mlp_bias', (D,)), ('up_bias', (FF,)), ('down_bias', (D,))]

def unpack(flat_vec):
    params = {}
    offset = 0
    for entry_name, entry_shape in layout():
        entry_count = math.prod(entry_shape)
        params[entry_name] = flat_vec[offset:offset + entry_count].reshape(entry_shape)
        offset = offset + entry_count
    return params

def pack_grads(grads):
    pieces = [grads[entry_name].reshape(-1) for entry_name, entry_shape in layout()]
    used_count = sum((math.prod(entry_shape) for entry_name, entry_shape in layout()))
    pieces.append(jnp.zeros((PARAMS - used_count,), jnp.float32))
    return jnp.concatenate(pieces)

def layer_norm(inputs, gain_vec, bias_vec):
    average = lax.optimization_barrier(jnp.mean(inputs, axis=-1, keepdims=True))
    centered = inputs - average
    variance = lax.optimization_barrier(jnp.mean(centered * centered, axis=-1, keepdims=True))
    return centered * lax.rsqrt(variance + NORM_EPS) * gain_vec + bias_vec

def forward(inputs, segment_ids, params):
    highest = lax.Precision.HIGHEST
    row_count = inputs.shape[0]
    normed_in = low(layer_norm(inputs, params['norm_gain'], params['norm_bias']))
    projected = low_back(jnp.dot(normed_in, params['qkv_weight'], precision=highest) + params['qkv_bias'])
    split_cols = projected.reshape(row_count, 3, HEADS, HD)
    queries = low(layer_norm(split_cols[:, 0], params['query_gain'], params['query_bias']))
    key_rows = low(layer_norm(split_cols[:, 1], params['key_gain'], params['key_bias']))
    value_rows = low(split_cols[:, 2])
    scores = low_back(jnp.einsum('qhd,khd->hqk', queries, key_rows, precision=highest) * HD ** (-0.5))
    same_image = segment_ids[:, None] == segment_ids[None, :]
    scores = jnp.where(same_image[None], scores, MASKED)
    attn_probs = jax.nn.softmax(scores, axis=-1)
    attended = jnp.einsum('hqk,khd->qhd', low(attn_probs), value_rows, precision=highest).reshape(row_count, D)
    attended = low(low_back(attended))
    branch = low_back(jnp.dot(attended, params['out_weight'], precision=highest) + params['out_bias'])
    residual = inputs + branch
    normed_mid = low(layer_norm(residual, params['mlp_gain'], params['mlp_bias']))
    hidden_pre = low_back(jnp.dot(normed_mid, params['up_weight'], precision=highest) + params['up_bias'])
    hidden_act = low(jax.nn.gelu(hidden_pre, approximate=False))
    return residual + jnp.dot(hidden_act, params['down_weight'], precision=highest) + params['down_bias']

def reference(patches, segments, out_grad, master, moment_one, moment_two):
    params = unpack(master.astype(jnp.bfloat16).astype(jnp.float32))

    def per_sequence(running, sequence_item):
        inputs, segment_ids, cotangent = sequence_item
        output, pull = jax.vjp(lambda values_in, weights_in: forward(values_in, segment_ids, weights_in), inputs.astype(jnp.float32), params)
        in_grad, weight_grads = pull(cotangent.astype(jnp.float32))
        return (running + pack_grads(weight_grads), (output.astype(jnp.bfloat16), in_grad.astype(jnp.bfloat16)))
    running, (activations, input_grad) = lax.scan(per_sequence, jnp.zeros((PARAMS,), jnp.float32), (patches, segments, out_grad))
    grad_sum = running / SEQS
    vector_grad = grad_sum[4 * D * D + 2 * D * FF:]
    first_moment = BETA_ONE * moment_one + (1.0 - BETA_ONE) * grad_sum
    second_moment = BETA_TWO * moment_two + (1.0 - BETA_TWO) * grad_sum * grad_sum
    first_hat = first_moment / (1.0 - BETA_ONE ** STEP)
    second_hat = second_moment / (1.0 - BETA_TWO ** STEP)
    positions = jnp.arange(PARAMS, dtype=jnp.int32)
    matrix_mask = (positions < 4 * D * D + 2 * D * FF).astype(jnp.float32)
    new_master = master - RATE * (first_hat / (jnp.sqrt(second_hat) + ADAM_EPS) + DECAY * matrix_mask * master)
    weights_copy = new_master.astype(jnp.bfloat16)
    return (activations, input_grad, grad_sum, vector_grad, new_master, first_moment, second_moment, weights_copy)
```

```python
import functools

import jax
import jax.numpy as jnp
from jax import lax
from jax.experimental import pallas as pl
from jax.experimental.pallas import tpu as pltpu
from jax.sharding import PartitionSpec as P

F32, BF16 = jnp.float32, jnp.bfloat16
MESH = pl.DeviceIdType.MESH
D, HEADS, HD, FF = 384, 6, 64, 1536
STEP = 3
PARAMS = 1775104
EPS = 1e-06
FAR = -1e30
BETA_ONE, BETA_TWO, RATE, DECAY, ADAM_EPS = 0.5, 0.5, 0.03, 0.1, 1e-08

LANES = 128
PAIRS = HEADS // 2
QKV_ROWS = 3 * D * D // LANES
OUT_ROWS = D * D // LANES
UP_ROWS = D * FF // LANES
MAT_ROWS = QKV_ROWS + OUT_ROWS + 2 * UP_ROWS
ALL_ROWS = PARAMS // LANES
QUARTER = ALL_ROWS // 4
KEPT = -(-QUARTER // 16) * 16
TAIL0 = QKV_ROWS
TAIL3 = 3408
VEC_AT = MAT_ROWS - 3 * QUARTER - TAIL3
NORM_GAIN, NORM_BIAS, QKV_BIAS, QUERY, KEY, OUT_BIAS, MLP_GAIN, MLP_BIAS, UP_BIAS, DOWN_BIAS = 0, 3, 6, 15, 16, 17, 20, 23, 26, 38
VMEM = 60 * 2**20


def dot(a, b):
    return jnp.dot(a, b, preferred_element_type=F32)


def dot_nt(a, b):
    return lax.dot_general(a, b, (((1,), (1,)), ((), ())), preferred_element_type=F32)


def dot_tn(a, b):
    return lax.dot_general(a, b, (((0,), (0,)), ((), ())), preferred_element_type=F32)


def row_of(vec, first, count):
    rows = [vec[VEC_AT + first + j : VEC_AT + first + j + 1, :] for j in range(count)]
    return jnp.concatenate(rows, axis=1) if count > 1 else rows[0]


def low_half(rows=1):
    return lax.broadcasted_iota(jnp.int32, (rows, LANES), 1) < HD


def both_halves(row, half):
    other = pltpu.roll(row, HD, 1)
    return jnp.where(low_half(), row, other) if half == 0 else jnp.where(low_half(), other, row)


def group_matrix(value, swapped=False):
    r = lax.rem(lax.broadcasted_iota(jnp.int32, (2 * LANES, LANES), 0), LANES) // HD
    c = lax.broadcasted_iota(jnp.int32, (2 * LANES, LANES), 1) // HD
    hit = (r != c) if swapped else (r == c)
    return jnp.where(hit, value, 0.0).astype(BF16)


def split(v):
    high = v.astype(BF16)
    return jnp.concatenate([high, (v - high.astype(F32)).astype(BF16)], axis=1)


def window(i, count):
    first, last = max(i - 1, 0), min(i + 2, count)
    return 256 * first, 256 * (last - first)


def columns(i, count):
    return sum(window(j, count)[1] for j in range(i))


def norm_stats(v):
    mean = jnp.mean(v, axis=1, keepdims=True)
    c = v - mean
    var = jnp.mean(c * c, axis=1, keepdims=True)
    r = lax.rsqrt(var + EPS)
    return c * r, r


def attn_forward_kernel(x_ref, qf_ref, kf_ref, w_ref, vec_ref, att_ref, e_ref, q_ref, k_ref, v_ref, xq_ref, xk_ref, rq_ref, rk_ref, it_ref, wp_ref, n_s, wf_s, ka_s, va_s):
    s, p = pl.program_id(0), pl.program_id(1)
    seq = x_ref.shape[1]
    blocks = seq // 256

    @pl.when((s == 0) & (p == 0))
    def _():
        wf_s[...] = w_ref[0, :QKV_ROWS].astype(F32)
        for j in range(PAIRS):
            for g in range(3):
                wp_ref[j, :, g * LANES : (g + 1) * LANES] = wf_s[pl.ds(3 * g + j, D, stride=9), :].astype(BF16)

    @pl.when(p == 0)
    def _():
        gain = row_of(vec_ref[...].astype(F32), NORM_GAIN, 3)
        bias = row_of(vec_ref[...].astype(F32), NORM_BIAS, 3)

        def body(i, carry):
            rows = pl.ds(pl.multiple_of(i * 256, 256), 256)
            xhat, _ = norm_stats(x_ref[0, rows, :].astype(F32))
            n_s[rows, :] = (xhat * gain + bias).astype(BF16)
            return carry

        lax.fori_loop(0, blocks, body, 0)

    vec = vec_ref[...].astype(F32)
    small = lax.broadcasted_iota(jnp.int32, (16, LANES), 0)
    qkv = vec[VEC_AT + QKV_BIAS : VEC_AT + QKV_BIAS + 9, :]
    which = lax.broadcasted_iota(jnp.int32, (9, LANES), 0)
    pick = lambda g: jnp.sum(jnp.where(which == 3 * g + p, qkv, 0.0), axis=0, keepdims=True)
    bias = jnp.concatenate([pick(0), pick(1), pick(2)], axis=1)
    qrow, krow = row_of(vec, QUERY, 1), row_of(vec, KEY, 1)
    qg, qb = both_halves(qrow, 0), both_halves(qrow, 1)
    kg, kb = both_halves(krow, 0), both_halves(krow, 1)
    means = group_matrix(1.0 / HD)
    w = wp_ref[p]

    def project(i, carry):
        rows = pl.ds(pl.multiple_of(i * 256, 256), 256)
        low = low_half(256)
        pr = dot(n_s[rows, :], w) + bias

        def head_norm(v):
            c = v - dot(split(v), means)
            r = lax.rsqrt(dot(split(c * c), means) + EPS)
            return c * r, r

        xq, rq = head_norm(pr[:, :LANES])
        xk, rk = head_norm(pr[:, LANES : 2 * LANES])
        q_ref[0, 0, rows, :] = ((xq * qg + qb) * HD**-0.5).astype(BF16)
        k = xk * kg + kb
        v = pr[:, 2 * LANES :]
        k_ref[0, 0, rows, :] = k.astype(BF16)
        v_ref[0, 0, rows, :] = v.astype(BF16)
        kf = kf_ref[0, rows, :].astype(F32)
        ka_s[0, rows, :] = jnp.where(low, k, kf).astype(BF16)
        ka_s[1, rows, :] = jnp.where(low, kf, k).astype(BF16)
        va_s[0, rows, :] = jnp.where(low, v, 1.0).astype(BF16)
        va_s[1, rows, :] = jnp.where(low, 1.0, v).astype(BF16)
        xq_ref[0, 0, rows, :] = xq.astype(BF16)
        xk_ref[0, 0, rows, :] = xk.astype(BF16)
        rq_ref[0, 0, rows, :] = rq
        rk_ref[0, 0, rows, :] = rk
        return carry

    lax.fori_loop(0, blocks, project, 0)

    low = low_half(256)
    for i in range(blocks):
        start, width = window(i, blocks)
        at = columns(i, blocks)
        rows = slice(256 * i, 256 * (i + 1))
        q = q_ref[0, 0, rows, :].astype(F32)
        qf = qf_ref[0, rows, :].astype(F32)
        sums = []
        for h in range(2):
            qa = (jnp.where(low, q, qf) if h == 0 else jnp.where(low, qf, q)).astype(BF16)
            scores = dot_nt(qa, ka_s[h, start : start + width, :])
            e = jnp.exp(scores - jnp.max(scores, axis=1, keepdims=True)).astype(BF16)
            e_ref[0, 0, 256 * h : 256 * (h + 1), at : at + width] = e
            sums.append(dot(e, va_s[h, start : start + width, :]))
        mixed = jnp.where(low, sums[0], sums[1])
        inverse = 1.0 / pltpu.roll(jnp.where(low, sums[1], sums[0]), HD, 1)
        att_ref[0, rows, :] = (mixed * inverse).astype(BF16)
        it_ref[0, 0, rows, :] = inverse


def attn_forward(x, qf, kf, weights, vec):
    seqs, seq, _ = x.shape
    total = columns(seq // 256, seq // 256)
    pair = lambda dtype: (jax.ShapeDtypeStruct((seqs, PAIRS, seq, LANES), dtype), pl.BlockSpec((1, 1, seq, LANES), lambda s, p: (s, p, 0, 0)))
    outs = [
        (jax.ShapeDtypeStruct((seqs, seq, D), BF16), pl.BlockSpec((1, seq, LANES), lambda s, p: (s, 0, p))),
        (jax.ShapeDtypeStruct((seqs, PAIRS, 512, total), BF16), pl.BlockSpec((1, 1, 512, total), lambda s, p: (s, p, 0, 0))),
        pair(BF16),
        pair(BF16),
        pair(BF16),
        pair(BF16),
        pair(BF16),
        pair(F32),
        pair(F32),
        pair(F32),
        (jax.ShapeDtypeStruct((PAIRS, D, D), BF16), pl.BlockSpec((PAIRS, D, D), lambda s, p: (0, 0, 0))),
    ]
    return pl.pallas_call(
        attn_forward_kernel,
        grid=(seqs, PAIRS),
        in_specs=[
            pl.BlockSpec((1, seq, D), lambda s, p: (s, 0, 0)),
            pl.BlockSpec((1, seq, LANES), lambda s, p: (s, 0, 0)),
            pl.BlockSpec((1, seq, LANES), lambda s, p: (s, 0, 0)),
            pl.BlockSpec((1, KEPT, LANES), lambda s, p: (0, 0, 0)),
            pl.BlockSpec(vec.shape, lambda s, p: (0, 0)),
        ],
        out_shape=[o[0] for o in outs],
        out_specs=[o[1] for o in outs],
        scratch_shapes=[
            pltpu.VMEM((seq, D), BF16),
            pltpu.VMEM((QKV_ROWS, LANES), F32),
            pltpu.VMEM((2, seq, LANES), BF16),
            pltpu.VMEM((2, seq, LANES), BF16),
        ],
        compiler_params=pltpu.CompilerParams(vmem_limit_bytes=VMEM),
        name="attn_forward",
    )(x, qf, kf, weights, vec)


def gelu_parts(x):
    bell = jnp.exp(x * x * -0.5)
    d = 1.0 + (0.3275911 * 0.5**0.5) * jnp.abs(x)
    t = pl.reciprocal(d, approx=True)
    t = t * (2.0 - d * t)
    poly = t * (0.127414796 + t * (-0.142248368 + t * (0.7107068705 + t * (-0.7265760135 + t * 0.5307027145))))
    tail = poly * bell
    share = jnp.where(x >= 0, 1.0 - tail, tail)
    return x * share, share + x * bell * 0.3989422804014327


def mlp_kernel(x_ref, att_ref, og_ref, w_ref, vec_ref, act_ref, mixed_ref, resid_ref, grads_ref, tail_ref, flat_s, wout_s, wup_s, wdown_s, mid_s, hid_s, pre_s, branch_s, colsum_s, upsum_s):
    t = pl.program_id(0)
    up_at, down_at = OUT_ROWS, OUT_ROWS + UP_ROWS
    step = KEPT // 7
    vec = vec_ref[...].astype(F32)
    tile = x_ref.shape[0]

    @pl.when(t == 0)
    def _():
        flat_s[0:16, :] = w_ref[0, TAIL0:KEPT].astype(F32)
        for k in range(1, 4):
            for c in range(7):
                at = k * QUARTER - QKV_ROWS + c * step
                count = min(step, flat_s.shape[0] - at)
                flat_s[at : at + count, :] = w_ref[k, c * step : (c + 1) * step].astype(F32)[:count]
        for j in range(3):
            wout_s[:, j * LANES : (j + 1) * LANES] = flat_s[pl.ds(j, D, stride=3), :].astype(BF16)
            wdown_s[:, j * LANES : (j + 1) * LANES] = flat_s[pl.ds(down_at + j, FF, stride=3), :].astype(BF16)
        for j in range(12):
            wup_s[:, j * LANES : (j + 1) * LANES] = flat_s[pl.ds(up_at + j, D, stride=12), :].astype(BF16)
        colsum_s[...] = jnp.zeros_like(colsum_s)
        upsum_s[...] = jnp.zeros_like(upsum_s)

    rows = pl.ds(pl.multiple_of(t * tile, tile), tile)
    fold = lambda v: jnp.sum(v.reshape(tile // 8, 8, v.shape[1]), axis=0)
    og = og_ref[rows, :]
    att = att_ref[rows, :]
    og_f = og.astype(F32)
    residual = x_ref[...].astype(F32) + dot(att, wout_s[...]) + row_of(vec, OUT_BIAS, 3)
    xhat, r = norm_stats(residual)
    gain = row_of(vec, MLP_GAIN, 3)
    mid = (xhat * gain + row_of(vec, MLP_BIAS, 3)).astype(BF16)
    mid_s[rows, :] = mid
    act = residual + row_of(vec, DOWN_BIAS, 3)
    mid_grad = jnp.zeros((tile, D), F32)
    wide = 512
    for c in range(FF // wide):
        cols = slice(c * wide, (c + 1) * wide)
        pre = dot(mid, wup_s[:, cols]) + row_of(vec, UP_BIAS + c * wide // LANES, wide // LANES)
        act_grad = dot_nt(og, wdown_s[cols, :])
        hidden, slope = gelu_parts(pre)
        hidden = hidden.astype(BF16)
        pre_grad = (act_grad * slope).astype(BF16)
        hid_s[rows, cols] = hidden
        pre_s[rows, cols] = pre_grad
        upsum_s[:, cols] += fold(pre_grad.astype(F32))
        act = act + dot(hidden, wdown_s[cols, :])
        mid_grad = mid_grad + dot_nt(pre_grad, wup_s[:, cols])
    act_ref[...] = act.astype(BF16)
    e_hat = mid_grad * gain
    resid = og_f + (e_hat - jnp.mean(e_hat, axis=1, keepdims=True) - xhat * jnp.mean(e_hat * xhat, axis=1, keepdims=True)) * r
    branch = resid.astype(BF16)
    resid_ref[...] = resid
    branch_s[rows, :] = branch
    mixed_ref[...] = dot_nt(branch, wout_s[...]).astype(BF16)
    colsum_s[0] += fold(og_f)
    colsum_s[1] += fold(mid_grad * xhat)
    colsum_s[2] += fold(mid_grad)
    colsum_s[3] += fold(branch.astype(F32))

    @pl.when(t == pl.num_programs(0) - 1)
    def _():
        for j in range(3):
            flat_s[pl.ds(j, D, stride=3), :] = dot_tn(att_ref[...], branch_s[:, j * LANES : (j + 1) * LANES])

        def ups(c, carry):
            g = dot_tn(mid_s[...], pre_s[:, pl.ds(pl.multiple_of(c * 256, 256), 256)])
            for j in range(2):
                flat_s[pl.ds(up_at + 2 * c + j, D, stride=12), :] = g[:, j * LANES : (j + 1) * LANES]
            return carry

        lax.fori_loop(0, FF // 256, ups, 0)

        def downs(c, carry):
            g = dot_tn(hid_s[:, pl.ds(pl.multiple_of(c * 256, 256), 256)], og_ref[...])
            for j in range(3):
                flat_s[pl.ds(down_at + 768 * c + j, 256, stride=3), :] = g[:, j * LANES : (j + 1) * LANES]
            return carry

        lax.fori_loop(0, FF // 256, downs, 0)
        sums = jnp.sum(colsum_s[...], axis=1)
        upsum = jnp.sum(upsum_s[...], axis=0, keepdims=True)
        vec_at = MAT_ROWS - QKV_ROWS
        flat_s[vec_at:, :] = jnp.zeros((flat_s.shape[0] - vec_at, LANES), F32)
        for j in range(3):
            part = slice(j * LANES, (j + 1) * LANES)
            flat_s[vec_at + DOWN_BIAS + j : vec_at + DOWN_BIAS + j + 1, :] = sums[0:1, part]
            flat_s[vec_at + MLP_GAIN + j : vec_at + MLP_GAIN + j + 1, :] = sums[1:2, part]
            flat_s[vec_at + MLP_BIAS + j : vec_at + MLP_BIAS + j + 1, :] = sums[2:3, part]
            flat_s[vec_at + OUT_BIAS + j : vec_at + OUT_BIAS + j + 1, :] = sums[3:4, part]
        for j in range(12):
            flat_s[vec_at + UP_BIAS + j : vec_at + UP_BIAS + j + 1, :] = upsum[:, j * LANES : (j + 1) * LANES]
        for k in range(1, 4):
            for c in range(7):
                at = k * QUARTER - QKV_ROWS + c * step
                grads_ref[k - 1, c * step : (c + 1) * step, :] = flat_s[at : at + step, :].astype(BF16)
        tail_ref[0:16, :] = flat_s[0:16, :]
        tail_ref[16:80, :] = flat_s[3 * QUARTER - QKV_ROWS + TAIL3 : 3 * QUARTER - QKV_ROWS + KEPT, :]


def mlp(x, att, og, weights, vec):
    tokens = x.shape[0]
    tile = 256
    padded = 3 * QUARTER + KEPT - QKV_ROWS
    tiled = pl.BlockSpec((tile, D), lambda t: (t, 0))
    whole = lambda *shape: pl.BlockSpec(shape, lambda t: (0,) * len(shape))
    return pl.pallas_call(
        mlp_kernel,
        grid=(tokens // tile,),
        in_specs=[tiled, whole(tokens, D), whole(tokens, D), whole(4, KEPT, LANES), whole(*vec.shape)],
        out_shape=[
            jax.ShapeDtypeStruct((tokens, D), BF16),
            jax.ShapeDtypeStruct((tokens, D), BF16),
            jax.ShapeDtypeStruct((tokens, D), F32),
            jax.ShapeDtypeStruct((3, KEPT, LANES), BF16),
            jax.ShapeDtypeStruct((80, LANES), F32),
        ],
        out_specs=[tiled, tiled, tiled, whole(3, KEPT, LANES), whole(80, LANES)],
        scratch_shapes=[
            pltpu.VMEM((padded, LANES), F32),
            pltpu.VMEM((D, D), BF16),
            pltpu.VMEM((D, FF), BF16),
            pltpu.VMEM((FF, D), BF16),
            pltpu.VMEM((tokens, D), BF16),
            pltpu.VMEM((tokens, FF), BF16),
            pltpu.VMEM((tokens, FF), BF16),
            pltpu.VMEM((tokens, D), BF16),
            pltpu.VMEM((4, 8, D), F32),
            pltpu.VMEM((8, FF), F32),
        ],
        compiler_params=pltpu.CompilerParams(vmem_limit_bytes=VMEM),
        name="mlp",
    )(x, att, og, weights, vec)


def attn_backward_kernel(x_ref, resid_ref, mixed_ref, att_ref, e_ref, q_ref, k_ref, v_ref, xq_ref, xk_ref, rq_ref, rk_ref, it_ref, wp_ref, vec_ref, tail_ref, gin_ref, grad_ref, tail_out_ref, n_s, in_s, dq_s, dk_s, dv_s, va_s, pg_s, acc_s, flat_s, sums_s, heads_s, bias_s):
    s, p = pl.program_id(0), pl.program_id(1)
    seq = x_ref.shape[1]
    blocks = seq // 256
    vec = vec_ref[...].astype(F32)
    fold = lambda v: jnp.sum(v.reshape(v.shape[0] // 8, 8, v.shape[1]), axis=0)
    low = low_half(256)

    @pl.when((s == 0) & (p == 0))
    def _():
        acc_s[...] = jnp.zeros_like(acc_s)
        sums_s[...] = jnp.zeros_like(sums_s)
        heads_s[...] = jnp.zeros_like(heads_s)
        bias_s[...] = jnp.zeros_like(bias_s)

    @pl.when(p == 0)
    def _():
        gain, bias = row_of(vec, NORM_GAIN, 3), row_of(vec, NORM_BIAS, 3)

        def body(i, carry):
            rows = pl.ds(pl.multiple_of(i * 256, 256), 256)
            xhat, _ = norm_stats(x_ref[0, rows, :].astype(F32))
            n_s[rows, :] = (xhat * gain + bias).astype(BF16)
            return carry

        lax.fori_loop(0, blocks, body, 0)

    dk_s[...] = jnp.zeros_like(dk_s)
    dv_s[...] = jnp.zeros_like(dv_s)
    ones = jnp.ones((256, LANES), F32)
    for i in range(blocks):
        rows = slice(256 * i, 256 * (i + 1))
        v = v_ref[0, 0, rows, :].astype(F32)
        va_s[0, rows, :] = jnp.where(low, v, ones).astype(BF16)
        va_s[1, rows, :] = jnp.where(low, ones, v).astype(BF16)
    swapped = group_matrix(1.0, swapped=True)
    lane = lax.rem(lax.broadcasted_iota(jnp.int32, (256, LANES), 1), HD)
    for i in range(blocks):
        start, width = window(i, blocks)
        at = columns(i, blocks)
        rows = slice(256 * i, 256 * (i + 1))
        keys = slice(start, start + width)
        do = (mixed_ref[0, rows, :].astype(F32) * it_ref[0, 0, rows, :]).astype(BF16).astype(F32)
        inner = dot(split(do * att_ref[0, rows, :].astype(F32)), swapped)
        high = inner.astype(BF16).astype(F32)
        extra = jnp.where(lane == 0, -high, jnp.where(lane == 1, high - inner, 0.0))
        q = q_ref[0, 0, rows, :].astype(F32)
        zero = jnp.zeros_like(q)
        dqs, dk, dv = [], None, None
        for h in range(2):
            mine = (lambda a, b: jnp.where(low, a, b).astype(BF16)) if h == 0 else (lambda a, b: jnp.where(low, b, a).astype(BF16))
            e = e_ref[0, 0, 256 * h : 256 * (h + 1), at : at + width]
            de = dot_nt(mine(do, extra), va_s[h, keys, :])
            ds = e * de.astype(BF16)
            dqs.append(dot(ds, k_ref[0, 0, keys, :]))
            dk_h = dot_tn(ds, mine(q, zero))
            dv_h = dot_tn(e, mine(do, zero))
            dk, dv = (dk_h, dv_h) if h == 0 else (dk + dk_h, dv + dv_h)
        dq_s[rows, :] = jnp.where(low, dqs[0], dqs[1]) * HD**-0.5
        dk_s[keys, :] += dk
        dv_s[keys, :] += dv

    qrow, krow = row_of(vec, QUERY, 1), row_of(vec, KEY, 1)
    qg, kg = both_halves(qrow, 0), both_halves(krow, 0)
    means = group_matrix(1.0 / HD)

    def pull(i, carry):
        rows = pl.ds(pl.multiple_of(i * 256, 256), 256)
        dq, dk, dv = dq_s[rows, :], dk_s[rows, :], dv_s[rows, :]

        def back(d, xhat, r, g):
            e_hat = d * g
            return (e_hat - dot(split(e_hat), means) - xhat * dot(split(e_hat * xhat), means)) * r

        xq, xk = xq_ref[0, 0, rows, :].astype(F32), xk_ref[0, 0, rows, :].astype(F32)
        heads_s[0] += fold(dq * xq)
        heads_s[1] += fold(dq)
        heads_s[2] += fold(dk * xk)
        heads_s[3] += fold(dk)
        pg = jnp.concatenate([back(dq, xq, rq_ref[0, 0, rows, :], qg), back(dk, xk, rk_ref[0, 0, rows, :], kg), dv], axis=1).astype(BF16)
        pg_s[rows, :] = pg
        bias_s[p] += fold(pg.astype(F32))
        share = dot_nt(pg, wp_ref[p])

        @pl.when(p == 0)
        def _():
            in_s[rows, :] = share

        @pl.when(p > 0)
        def _():
            in_s[rows, :] += share

        return carry

    lax.fori_loop(0, blocks, pull, 0)
    acc_s[p] += dot_tn(n_s[...], pg_s[...])

    @pl.when(p == PAIRS - 1)
    def _():
        gain = row_of(vec, NORM_GAIN, 3)

        def body(i, carry):
            rows = pl.ds(pl.multiple_of(i * 256, 256), 256)
            xhat, r = norm_stats(x_ref[0, rows, :].astype(F32))
            d = in_s[rows, :]
            e_hat = d * gain
            back = (e_hat - jnp.mean(e_hat, axis=1, keepdims=True) - xhat * jnp.mean(e_hat * xhat, axis=1, keepdims=True)) * r
            gin_ref[0, rows, :] = (resid_ref[0, rows, :] + back).astype(BF16)
            sums_s[0] += fold(d * xhat)
            sums_s[1] += fold(d)
            return carry

        lax.fori_loop(0, blocks, body, 0)

    @pl.when((s == pl.num_programs(0) - 1) & (p == PAIRS - 1))
    def _():
        for j in range(PAIRS):
            for g in range(3):
                flat_s[pl.ds(3 * g + j, D, stride=9), :] = acc_s[j, :, g * LANES : (g + 1) * LANES]
        grad_ref[0:TAIL0, :] = flat_s[...].astype(BF16)
        grad_ref[TAIL0:KEPT, :] = tail_ref[0:16, :].astype(BF16)
        tail_out_ref[...] = tail_ref[16:80, :]
        sums = jnp.sum(sums_s[...], axis=1)
        heads = jnp.sum(heads_s[...], axis=1)
        heads = heads + pltpu.roll(heads, HD, 1)
        biases = jnp.sum(bias_s[...], axis=1)

        def put(row, value):
            tail_out_ref[VEC_AT + row : VEC_AT + row + 1, :] = value

        for j in range(3):
            part = slice(j * LANES, (j + 1) * LANES)
            put(NORM_GAIN + j, sums[0:1, part])
            put(NORM_BIAS + j, sums[1:2, part])
            for g in range(3):
                put(QKV_BIAS + 3 * g + j, biases[j : j + 1, g * LANES : (g + 1) * LANES])
        put(QUERY, jnp.where(low_half(), heads[0:1], heads[1:2]))
        put(KEY, jnp.where(low_half(), heads[2:3], heads[3:4]))


def attn_backward(x, resid, mixed, att, e, q, k, v, xq, xk, rq, rk, it, wp, vec, tail):
    seqs, seq, _ = x.shape
    total = e.shape[-1]
    pair = pl.BlockSpec((1, 1, seq, LANES), lambda s, p: (s, p, 0, 0))
    whole = lambda *shape: pl.BlockSpec(shape, lambda s, p: (0,) * len(shape))
    full = pl.BlockSpec((1, seq, D), lambda s, p: (s, 0, 0))
    return pl.pallas_call(
        attn_backward_kernel,
        grid=(seqs, PAIRS),
        in_specs=[
            full,
            full,
            pl.BlockSpec((1, seq, LANES), lambda s, p: (s, 0, p)),
            pl.BlockSpec((1, seq, LANES), lambda s, p: (s, 0, p)),
            pl.BlockSpec((1, 1, 512, total), lambda s, p: (s, p, 0, 0)),
            pair,
            pair,
            pair,
            pair,
            pair,
            pair,
            pair,
            pair,
            whole(PAIRS, D, D),
            whole(*vec.shape),
            whole(80, LANES),
        ],
        out_shape=[
            jax.ShapeDtypeStruct((seqs, seq, D), BF16),
            jax.ShapeDtypeStruct((KEPT, LANES), BF16),
            jax.ShapeDtypeStruct((64, LANES), F32),
        ],
        out_specs=[full, whole(KEPT, LANES), whole(64, LANES)],
        scratch_shapes=[
            pltpu.VMEM((seq, D), BF16),
            pltpu.VMEM((seq, D), F32),
            pltpu.VMEM((seq, LANES), F32),
            pltpu.VMEM((seq, LANES), F32),
            pltpu.VMEM((seq, LANES), F32),
            pltpu.VMEM((2, seq, LANES), BF16),
            pltpu.VMEM((seq, D), BF16),
            pltpu.VMEM((PAIRS, D, D), F32),
            pltpu.VMEM((QKV_ROWS, LANES), F32),
            pltpu.VMEM((2, 8, D), F32),
            pltpu.VMEM((4, 8, LANES), F32),
            pltpu.VMEM((PAIRS, 8, D), F32),
        ],
        compiler_params=pltpu.CompilerParams(vmem_limit_bytes=VMEM),
        name="attn_backward",
    )(x, resid, mixed, att, e, q, k, v, xq, xk, rq, rk, it, wp, vec, tail)


def shards(patches, segments, out_grad, master, moment_one, moment_two):
    seqs, seq, _ = patches.shape
    rows = master.reshape(QUARTER, LANES).astype(BF16)
    rows = jnp.pad(rows, ((0, KEPT - QUARTER), (0, 0)))
    weights = lax.all_gather(rows, "shard", axis=0, tiled=False)
    vec = weights[3, TAIL3:KEPT]
    slot = jnp.arange(LANES, dtype=jnp.int32) % HD
    same = segments[:, :, None] == slot
    qf = jnp.where((slot < 8) & ~same, 1.0, 0.0).astype(BF16)
    kf = jnp.where((slot < 8) & same, FAR, 0.0).astype(BF16)
    att, e, q, k, v, xq, xk, rq, rk, it, wp = attn_forward(patches, qf, kf, weights, vec)
    flat = lambda a: a.reshape(seqs * seq, D)
    act, mixed, resid, grads, tail = mlp(flat(patches), flat(att), flat(out_grad), weights, vec)
    whole = lambda a: a.reshape(seqs, seq, D)
    input_grad, first, vec_tail = attn_backward(patches, whole(resid), whole(mixed), att, e, q, k, v, xq, xk, rq, rk, it, wp, vec, tail)
    sequences = seqs * lax.axis_size("dp") * lax.axis_size("shard")
    grads = grads.at[2, TAIL3:].set(vec_tail.astype(BF16))
    grads = jnp.concatenate([first[None], grads], axis=0)
    vector_grad = lax.psum(vec_tail, ("dp", "shard"))[VEC_AT : VEC_AT + ALL_ROWS - MAT_ROWS].reshape(-1) / sequences
    owned = lax.psum_scatter(grads, "shard", scatter_dimension=0, tiled=False).astype(F32)
    owned = lax.psum(owned, "dp")
    grad_sum = owned[:QUARTER].reshape(-1) / sequences
    first_moment = BETA_ONE * moment_one + (1.0 - BETA_ONE) * grad_sum
    second_moment = BETA_TWO * moment_two + (1.0 - BETA_TWO) * grad_sum * grad_sum
    first_hat = first_moment / (1.0 - BETA_ONE**STEP)
    second_hat = second_moment / (1.0 - BETA_TWO**STEP)
    positions = lax.axis_index("shard") * QUARTER * LANES + jnp.arange(QUARTER * LANES, dtype=jnp.int32)
    mask = (positions < MAT_ROWS * LANES).astype(F32)
    new_master = master - RATE * (first_hat / (jnp.sqrt(second_hat) + ADAM_EPS) + DECAY * mask * master)
    weights_copy = lax.all_gather(new_master.astype(BF16), "shard", axis=0, tiled=True)
    return whole(act), input_grad, grad_sum, vector_grad, new_master, first_moment, second_moment, weights_copy


def solution(mesh):
    split_rows = P(("dp", "shard"), None, None)
    return jax.shard_map(
        shards,
        mesh=mesh,
        in_specs=(split_rows, P(("dp", "shard"), None), split_rows, P("shard"), P("shard"), P("shard")),
        out_specs=(split_rows, split_rows, P("shard"), P(), P("shard"), P("shard"), P("shard"), P()),
        check_vma=False,
    )
```

```python
import functools

import jax
import jax.numpy as jnp
from jax import lax
from jax.experimental import pallas as pl
from jax.experimental.pallas import tpu as pltpu
from jax.sharding import PartitionSpec as P

F32, BF16 = jnp.float32, jnp.bfloat16
MESH = pl.DeviceIdType.MESH
D, HEADS, HD, FF = 384, 6, 64, 1536
STEP = 3
PARAMS = 1775104
EPS = 1e-06
FAR = -1e30
BETA_ONE, BETA_TWO, RATE, DECAY, ADAM_EPS = 0.5, 0.5, 0.03, 0.1, 1e-08

LANES = 128
PAIRS = HEADS // 2
QKV_ROWS = 3 * D * D // LANES
OUT_ROWS = D * D // LANES
UP_ROWS = D * FF // LANES
MAT_ROWS = QKV_ROWS + OUT_ROWS + 2 * UP_ROWS
ALL_ROWS = PARAMS // LANES
QUARTER = ALL_ROWS // 4
KEPT = -(-QUARTER // 16) * 16
TAIL0 = QKV_ROWS
TAIL3 = 3408
VEC_AT = MAT_ROWS - 3 * QUARTER - TAIL3
NORM_GAIN, NORM_BIAS, QKV_BIAS, QUERY, KEY, OUT_BIAS, MLP_GAIN, MLP_BIAS, UP_BIAS, DOWN_BIAS = 0, 3, 6, 15, 16, 17, 20, 23, 26, 38
VMEM = 60 * 2**20


def dot(a, b):
    return jnp.dot(a, b, preferred_element_type=F32)


def dot_nt(a, b):
    return lax.dot_general(a, b, (((1,), (1,)), ((), ())), preferred_element_type=F32)


def dot_tn(a, b):
    return lax.dot_general(a, b, (((0,), (0,)), ((), ())), preferred_element_type=F32)


def row_of(vec, first, count):
    rows = [vec[VEC_AT + first + j : VEC_AT + first + j + 1, :] for j in range(count)]
    return jnp.concatenate(rows, axis=1) if count > 1 else rows[0]


def low_half(rows=1):
    return lax.broadcasted_iota(jnp.int32, (rows, LANES), 1) < HD


def both_halves(row, half):
    other = pltpu.roll(row, HD, 1)
    return jnp.where(low_half(), row, other) if half == 0 else jnp.where(low_half(), other, row)


def group_matrix(value, swapped=False):
    r = lax.rem(lax.broadcasted_iota(jnp.int32, (2 * LANES, LANES), 0), LANES) // HD
    c = lax.broadcasted_iota(jnp.int32, (2 * LANES, LANES), 1) // HD
    hit = (r != c) if swapped else (r == c)
    return jnp.where(hit, value, 0.0).astype(BF16)


def split(v):
    high = v.astype(BF16)
    return jnp.concatenate([high, (v - high.astype(F32)).astype(BF16)], axis=1)


def window(i, count):
    first, last = max(i - 1, 0), min(i + 2, count)
    return 256 * first, 256 * (last - first)


def columns(i, count):
    return sum(window(j, count)[1] for j in range(i))


def norm_stats(v):
    mean = jnp.mean(v, axis=1, keepdims=True)
    c = v - mean
    var = jnp.mean(c * c, axis=1, keepdims=True)
    r = lax.rsqrt(var + EPS)
    return c * r, r


def attn_forward_kernel(x_ref, qf_ref, kf_ref, w_ref, vec_ref, att_ref, e_ref, q_ref, k_ref, v_ref, xq_ref, xk_ref, rq_ref, rk_ref, it_ref, wp_ref, n_s, wf_s, ka_s, va_s):
    s, p = pl.program_id(0), pl.program_id(1)
    seq = x_ref.shape[1]
    blocks = seq // 256

    @pl.when((s == 0) & (p == 0))
    def _():
        wf_s[...] = w_ref[0, :QKV_ROWS].astype(F32)
        for j in range(PAIRS):
            for g in range(3):
                wp_ref[j, :, g * LANES : (g + 1) * LANES] = wf_s[pl.ds(3 * g + j, D, stride=9), :].astype(BF16)

    @pl.when(p == 0)
    def _():
        gain = row_of(vec_ref[...].astype(F32), NORM_GAIN, 3)
        bias = row_of(vec_ref[...].astype(F32), NORM_BIAS, 3)

        def body(i, carry):
            rows = pl.ds(pl.multiple_of(i * 256, 256), 256)
            xhat, _ = norm_stats(x_ref[0, rows, :].astype(F32))
            n_s[rows, :] = (xhat * gain + bias).astype(BF16)
            return carry

        lax.fori_loop(0, blocks, body, 0)

    vec = vec_ref[...].astype(F32)
    small = lax.broadcasted_iota(jnp.int32, (16, LANES), 0)
    qkv = vec[VEC_AT + QKV_BIAS : VEC_AT + QKV_BIAS + 9, :]
    which = lax.broadcasted_iota(jnp.int32, (9, LANES), 0)
    pick = lambda g: jnp.sum(jnp.where(which == 3 * g + p, qkv, 0.0), axis=0, keepdims=True)
    bias = jnp.concatenate([pick(0), pick(1), pick(2)], axis=1)
    qrow, krow = row_of(vec, QUERY, 1), row_of(vec, KEY, 1)
    qg, qb = both_halves(qrow, 0), both_halves(qrow, 1)
    kg, kb = both_halves(krow, 0), both_halves(krow, 1)
    means = group_matrix(1.0 / HD)
    w = wp_ref[p]

    def project(i, carry):
        rows = pl.ds(pl.multiple_of(i * 256, 256), 256)
        low = low_half(256)
        pr = dot(n_s[rows, :], w) + bias

        def head_norm(v):
            c = v - dot(split(v), means)
            r = lax.rsqrt(dot(split(c * c), means) + EPS)
            return c * r, r

        xq, rq = head_norm(pr[:, :LANES])
        xk, rk = head_norm(pr[:, LANES : 2 * LANES])
        q_ref[0, 0, rows, :] = ((xq * qg + qb) * HD**-0.5).astype(BF16)
        k = xk * kg + kb
        v = pr[:, 2 * LANES :]
        k_ref[0, 0, rows, :] = k.astype(BF16)
        v_ref[0, 0, rows, :] = v.astype(BF16)
        kf = kf_ref[0, rows, :].astype(F32)
        ka_s[0, rows, :] = jnp.where(low, k, kf).astype(BF16)
        ka_s[1, rows, :] = jnp.where(low, kf, k).astype(BF16)
        va_s[0, rows, :] = jnp.where(low, v, 1.0).astype(BF16)
        va_s[1, rows, :] = jnp.where(low, 1.0, v).astype(BF16)
        xq_ref[0, 0, rows, :] = xq.astype(BF16)
        xk_ref[0, 0, rows, :] = xk.astype(BF16)
        rq_ref[0, 0, rows, :] = rq
        rk_ref[0, 0, rows, :] = rk
        return carry

    lax.fori_loop(0, blocks, project, 0)

    low = low_half(256)
    for i in range(blocks):
        start, width = window(i, blocks)
        at = columns(i, blocks)
        rows = slice(256 * i, 256 * (i + 1))
        q = q_ref[0, 0, rows, :].astype(F32)
        qf = qf_ref[0, rows, :].astype(F32)
        sums = []
        for h in range(2):
            qa = (jnp.where(low, q, qf) if h == 0 else jnp.where(low, qf, q)).astype(BF16)
            scores = dot_nt(qa, ka_s[h, start : start + width, :])
            e = jnp.exp(scores - jnp.max(scores, axis=1, keepdims=True)).astype(BF16)
            e_ref[0, 0, 256 * h : 256 * (h + 1), at : at + width] = e
            sums.append(dot(e, va_s[h, start : start + width, :]))
        mixed = jnp.where(low, sums[0], sums[1])
        inverse = 1.0 / pltpu.roll(jnp.where(low, sums[1], sums[0]), HD, 1)
        att_ref[0, rows, :] = (mixed * inverse).astype(BF16)
        it_ref[0, 0, rows, :] = inverse


def attn_forward(x, qf, kf, weights, vec):
    seqs, seq, _ = x.shape
    total = columns(seq // 256, seq // 256)
    pair = lambda dtype: (jax.ShapeDtypeStruct((seqs, PAIRS, seq, LANES), dtype), pl.BlockSpec((1, 1, seq, LANES), lambda s, p: (s, p, 0, 0)))
    outs = [
        (jax.ShapeDtypeStruct((seqs, seq, D), BF16), pl.BlockSpec((1, seq, LANES), lambda s, p: (s, 0, p))),
        (jax.ShapeDtypeStruct((seqs, PAIRS, 512, total), BF16), pl.BlockSpec((1, 1, 512, total), lambda s, p: (s, p, 0, 0))),
        pair(BF16),
        pair(BF16),
        pair(BF16),
        pair(BF16),
        pair(BF16),
        pair(F32),
        pair(F32),
        pair(F32),
        (jax.ShapeDtypeStruct((PAIRS, D, D), BF16), pl.BlockSpec((PAIRS, D, D), lambda s, p: (0, 0, 0))),
    ]
    return pl.pallas_call(
        attn_forward_kernel,
        grid=(seqs, PAIRS),
        in_specs=[
            pl.BlockSpec((1, seq, D), lambda s, p: (s, 0, 0)),
            pl.BlockSpec((1, seq, LANES), lambda s, p: (s, 0, 0)),
            pl.BlockSpec((1, seq, LANES), lambda s, p: (s, 0, 0)),
            pl.BlockSpec((1, QKV_ROWS, LANES), lambda s, p: (0, 0, 0)),
            pl.BlockSpec(vec.shape, lambda s, p: (0, 0)),
        ],
        out_shape=[o[0] for o in outs],
        out_specs=[o[1] for o in outs],
        scratch_shapes=[
            pltpu.VMEM((seq, D), BF16),
            pltpu.VMEM((QKV_ROWS, LANES), F32),
            pltpu.VMEM((2, seq, LANES), BF16),
            pltpu.VMEM((2, seq, LANES), BF16),
        ],
        compiler_params=pltpu.CompilerParams(vmem_limit_bytes=VMEM),
        name="attn_forward",
    )(x, qf, kf, weights, vec)


def gelu_parts(x):
    bell = jnp.exp(x * x * -0.5)
    d = 1.0 + (0.3275911 * 0.5**0.5) * jnp.abs(x)
    t = pl.reciprocal(d, approx=True)
    t = t * (2.0 - d * t)
    poly = t * (0.127414796 + t * (-0.142248368 + t * (0.7107068705 + t * (-0.7265760135 + t * 0.5307027145))))
    tail = poly * bell
    share = jnp.where(x >= 0, 1.0 - tail, tail)
    return x * share, share + x * bell * 0.3989422804014327


def mlp_kernel(x_ref, att_ref, og_ref, w_ref, vec_ref, act_ref, mixed_ref, resid_ref, grads_ref, tail_ref, flat_s, wout_s, wup_s, wdown_s, mid_s, hid_s, pre_s, branch_s, colsum_s, upsum_s):
    t = pl.program_id(0)
    up_at, down_at = OUT_ROWS, OUT_ROWS + UP_ROWS
    step = KEPT // 7
    vec = vec_ref[...].astype(F32)
    tile = x_ref.shape[0]

    @pl.when(t == 0)
    def _():
        flat_s[0:16, :] = w_ref[0, TAIL0:KEPT].astype(F32)
        for k in range(1, 4):
            for c in range(7):
                at = k * QUARTER - QKV_ROWS + c * step
                count = min(step, flat_s.shape[0] - at)
                flat_s[at : at + count, :] = w_ref[k, c * step : (c + 1) * step].astype(F32)[:count]
        for j in range(3):
            wout_s[:, j * LANES : (j + 1) * LANES] = flat_s[pl.ds(j, D, stride=3), :].astype(BF16)
            wdown_s[:, j * LANES : (j + 1) * LANES] = flat_s[pl.ds(down_at + j, FF, stride=3), :].astype(BF16)
        for j in range(12):
            wup_s[:, j * LANES : (j + 1) * LANES] = flat_s[pl.ds(up_at + j, D, stride=12), :].astype(BF16)
        colsum_s[...] = jnp.zeros_like(colsum_s)
        upsum_s[...] = jnp.zeros_like(upsum_s)

    rows = pl.ds(pl.multiple_of(t * tile, tile), tile)
    fold = lambda v: jnp.sum(v.reshape(tile // 8, 8, v.shape[1]), axis=0)
    og = og_ref[rows, :]
    att = att_ref[rows, :]
    og_f = og.astype(F32)
    residual = x_ref[...].astype(F32) + dot(att, wout_s[...]) + row_of(vec, OUT_BIAS, 3)
    xhat, r = norm_stats(residual)
    gain = row_of(vec, MLP_GAIN, 3)
    mid = (xhat * gain + row_of(vec, MLP_BIAS, 3)).astype(BF16)
    mid_s[rows, :] = mid
    act = residual + row_of(vec, DOWN_BIAS, 3)
    mid_grad = jnp.zeros((tile, D), F32)
    wide = 512
    for c in range(FF // wide):
        cols = slice(c * wide, (c + 1) * wide)
        pre = dot(mid, wup_s[:, cols]) + row_of(vec, UP_BIAS + c * wide // LANES, wide // LANES)
        act_grad = dot_nt(og, wdown_s[cols, :])
        hidden, slope = gelu_parts(pre)
        hidden = hidden.astype(BF16)
        pre_grad = (act_grad * slope).astype(BF16)
        hid_s[rows, cols] = hidden
        pre_s[rows, cols] = pre_grad
        upsum_s[:, cols] += fold(pre_grad.astype(F32))
        act = act + dot(hidden, wdown_s[cols, :])
        mid_grad = mid_grad + dot_nt(pre_grad, wup_s[:, cols])
    act_ref[...] = act.astype(BF16)
    e_hat = mid_grad * gain
    resid = og_f + (e_hat - jnp.mean(e_hat, axis=1, keepdims=True) - xhat * jnp.mean(e_hat * xhat, axis=1, keepdims=True)) * r
    branch = resid.astype(BF16)
    resid_ref[...] = resid
    branch_s[rows, :] = branch
    mixed_ref[...] = dot_nt(branch, wout_s[...]).astype(BF16)
    colsum_s[0] += fold(og_f)
    colsum_s[1] += fold(mid_grad * xhat)
    colsum_s[2] += fold(mid_grad)
    colsum_s[3] += fold(branch.astype(F32))

    @pl.when(t == pl.num_programs(0) - 1)
    def _():
        for j in range(3):
            flat_s[pl.ds(j, D, stride=3), :] = dot_tn(att_ref[...], branch_s[:, j * LANES : (j + 1) * LANES])

        def ups(c, carry):
            g = dot_tn(mid_s[...], pre_s[:, pl.ds(pl.multiple_of(c * 256, 256), 256)])
            for j in range(2):
                flat_s[pl.ds(up_at + 2 * c + j, D, stride=12), :] = g[:, j * LANES : (j + 1) * LANES]
            return carry

        lax.fori_loop(0, FF // 256, ups, 0)

        def downs(c, carry):
            g = dot_tn(hid_s[:, pl.ds(pl.multiple_of(c * 256, 256), 256)], og_ref[...])
            for j in range(3):
                flat_s[pl.ds(down_at + 768 * c + j, 256, stride=3), :] = g[:, j * LANES : (j + 1) * LANES]
            return carry

        lax.fori_loop(0, FF // 256, downs, 0)
        sums = jnp.sum(colsum_s[...], axis=1)
        upsum = jnp.sum(upsum_s[...], axis=0, keepdims=True)
        vec_at = MAT_ROWS - QKV_ROWS
        flat_s[vec_at:, :] = jnp.zeros((flat_s.shape[0] - vec_at, LANES), F32)
        for j in range(3):
            part = slice(j * LANES, (j + 1) * LANES)
            flat_s[vec_at + DOWN_BIAS + j : vec_at + DOWN_BIAS + j + 1, :] = sums[0:1, part]
            flat_s[vec_at + MLP_GAIN + j : vec_at + MLP_GAIN + j + 1, :] = sums[1:2, part]
            flat_s[vec_at + MLP_BIAS + j : vec_at + MLP_BIAS + j + 1, :] = sums[2:3, part]
            flat_s[vec_at + OUT_BIAS + j : vec_at + OUT_BIAS + j + 1, :] = sums[3:4, part]
        for j in range(12):
            flat_s[vec_at + UP_BIAS + j : vec_at + UP_BIAS + j + 1, :] = upsum[:, j * LANES : (j + 1) * LANES]
        for k in range(1, 4):
            for c in range(7):
                at = k * QUARTER - QKV_ROWS + c * step
                grads_ref[k, c * step : (c + 1) * step, :] = flat_s[at : at + step, :].astype(BF16)
            if grads_ref.shape[1] > KEPT:
                grads_ref[k, KEPT:, :] = jnp.zeros((grads_ref.shape[1] - KEPT, LANES), BF16)
        tail_ref[0:16, :] = flat_s[0:16, :]
        tail_ref[16:80, :] = flat_s[3 * QUARTER - QKV_ROWS + TAIL3 : 3 * QUARTER - QKV_ROWS + KEPT, :]


def mlp(x, att, og, weights, vec):
    tokens = x.shape[0]
    tile = 256
    padded = 3 * QUARTER + KEPT - QKV_ROWS
    tiled = pl.BlockSpec((tile, D), lambda t: (t, 0))
    whole = lambda *shape: pl.BlockSpec(shape, lambda t: (0,) * len(shape))
    return pl.pallas_call(
        mlp_kernel,
        grid=(tokens // tile,),
        in_specs=[tiled, whole(tokens, D), whole(tokens, D), whole(*weights.shape), whole(*vec.shape)],
        out_shape=[
            jax.ShapeDtypeStruct((tokens, D), BF16),
            jax.ShapeDtypeStruct((tokens, D), BF16),
            jax.ShapeDtypeStruct((tokens, D), F32),
            jax.ShapeDtypeStruct(weights.shape, BF16),
            jax.ShapeDtypeStruct((80, LANES), F32),
        ],
        out_specs=[tiled, tiled, tiled, whole(*weights.shape), whole(80, LANES)],
        scratch_shapes=[
            pltpu.VMEM((padded, LANES), F32),
            pltpu.VMEM((D, D), BF16),
            pltpu.VMEM((D, FF), BF16),
            pltpu.VMEM((FF, D), BF16),
            pltpu.VMEM((tokens, D), BF16),
            pltpu.VMEM((tokens, FF), BF16),
            pltpu.VMEM((tokens, FF), BF16),
            pltpu.VMEM((tokens, D), BF16),
            pltpu.VMEM((4, 8, D), F32),
            pltpu.VMEM((8, FF), F32),
        ],
        compiler_params=pltpu.CompilerParams(vmem_limit_bytes=VMEM),
        name="mlp",
    )(x, att, og, weights, vec)


def attn_backward_kernel(x_ref, resid_ref, mixed_ref, att_ref, e_ref, q_ref, k_ref, v_ref, xq_ref, xk_ref, rq_ref, rk_ref, it_ref, wp_ref, vec_ref, tail_ref, old_ref, gin_ref, grads_ref, n_s, in_s, dq_s, dk_s, dv_s, va_s, pg_s, acc_s, flat_s, sums_s, heads_s, bias_s, first_s, tail_s, low_s, sems):
    s, p = pl.program_id(0), pl.program_id(1)
    seq = x_ref.shape[1]
    blocks = seq // 256
    vec = vec_ref[...].astype(F32)
    fold = lambda v: jnp.sum(v.reshape(v.shape[0] // 8, 8, v.shape[1]), axis=0)
    low = low_half(256)

    @pl.when((s == 0) & (p == 0))
    def _():
        acc_s[...] = jnp.zeros_like(acc_s)
        sums_s[...] = jnp.zeros_like(sums_s)
        heads_s[...] = jnp.zeros_like(heads_s)
        bias_s[...] = jnp.zeros_like(bias_s)

    @pl.when(p == 0)
    def _():
        gain, bias = row_of(vec, NORM_GAIN, 3), row_of(vec, NORM_BIAS, 3)

        def body(i, carry):
            rows = pl.ds(pl.multiple_of(i * 256, 256), 256)
            xhat, _ = norm_stats(x_ref[0, rows, :].astype(F32))
            n_s[rows, :] = (xhat * gain + bias).astype(BF16)
            return carry

        lax.fori_loop(0, blocks, body, 0)

    dk_s[...] = jnp.zeros_like(dk_s)
    dv_s[...] = jnp.zeros_like(dv_s)
    ones = jnp.ones((256, LANES), F32)
    for i in range(blocks):
        rows = slice(256 * i, 256 * (i + 1))
        v = v_ref[0, 0, rows, :].astype(F32)
        va_s[0, rows, :] = jnp.where(low, v, ones).astype(BF16)
        va_s[1, rows, :] = jnp.where(low, ones, v).astype(BF16)
    swapped = group_matrix(1.0, swapped=True)
    lane = lax.rem(lax.broadcasted_iota(jnp.int32, (256, LANES), 1), HD)
    for i in range(blocks):
        start, width = window(i, blocks)
        at = columns(i, blocks)
        rows = slice(256 * i, 256 * (i + 1))
        keys = slice(start, start + width)
        do = (mixed_ref[0, rows, :].astype(F32) * it_ref[0, 0, rows, :]).astype(BF16).astype(F32)
        inner = dot(split(do * att_ref[0, rows, :].astype(F32)), swapped)
        high = inner.astype(BF16).astype(F32)
        extra = jnp.where(lane == 0, -high, jnp.where(lane == 1, high - inner, 0.0))
        q = q_ref[0, 0, rows, :].astype(F32)
        zero = jnp.zeros_like(q)
        dqs, dk, dv = [], None, None
        for h in range(2):
            mine = (lambda a, b: jnp.where(low, a, b).astype(BF16)) if h == 0 else (lambda a, b: jnp.where(low, b, a).astype(BF16))
            e = e_ref[0, 0, 256 * h : 256 * (h + 1), at : at + width]
            de = dot_nt(mine(do, extra), va_s[h, keys, :])
            ds = e * de.astype(BF16)
            dqs.append(dot(ds, k_ref[0, 0, keys, :]))
            dk_h = dot_tn(ds, mine(q, zero))
            dv_h = dot_tn(e, mine(do, zero))
            dk, dv = (dk_h, dv_h) if h == 0 else (dk + dk_h, dv + dv_h)
        dq_s[rows, :] = jnp.where(low, dqs[0], dqs[1]) * HD**-0.5
        dk_s[keys, :] += dk
        dv_s[keys, :] += dv

    qrow, krow = row_of(vec, QUERY, 1), row_of(vec, KEY, 1)
    qg, kg = both_halves(qrow, 0), both_halves(krow, 0)
    means = group_matrix(1.0 / HD)

    def pull(i, carry):
        rows = pl.ds(pl.multiple_of(i * 256, 256), 256)
        dq, dk, dv = dq_s[rows, :], dk_s[rows, :], dv_s[rows, :]

        def back(d, xhat, r, g):
            e_hat = d * g
            return (e_hat - dot(split(e_hat), means) - xhat * dot(split(e_hat * xhat), means)) * r

        xq, xk = xq_ref[0, 0, rows, :].astype(F32), xk_ref[0, 0, rows, :].astype(F32)
        heads_s[0] += fold(dq * xq)
        heads_s[1] += fold(dq)
        heads_s[2] += fold(dk * xk)
        heads_s[3] += fold(dk)
        pg = jnp.concatenate([back(dq, xq, rq_ref[0, 0, rows, :], qg), back(dk, xk, rk_ref[0, 0, rows, :], kg), dv], axis=1).astype(BF16)
        pg_s[rows, :] = pg
        bias_s[p] += fold(pg.astype(F32))
        share = dot_nt(pg, wp_ref[p])

        @pl.when(p == 0)
        def _():
            in_s[rows, :] = share

        @pl.when(p > 0)
        def _():
            in_s[rows, :] += share

        return carry

    lax.fori_loop(0, blocks, pull, 0)
    acc_s[p] += dot_tn(n_s[...], pg_s[...])

    @pl.when(p == PAIRS - 1)
    def _():
        gain = row_of(vec, NORM_GAIN, 3)

        def body(i, carry):
            rows = pl.ds(pl.multiple_of(i * 256, 256), 256)
            xhat, r = norm_stats(x_ref[0, rows, :].astype(F32))
            d = in_s[rows, :]
            e_hat = d * gain
            back = (e_hat - jnp.mean(e_hat, axis=1, keepdims=True) - xhat * jnp.mean(e_hat * xhat, axis=1, keepdims=True)) * r
            gin_ref[0, rows, :] = (resid_ref[0, rows, :] + back).astype(BF16)
            sums_s[0] += fold(d * xhat)
            sums_s[1] += fold(d)
            return carry

        lax.fori_loop(0, blocks, body, 0)

    @pl.when((s == pl.num_programs(0) - 1) & (p == PAIRS - 1))
    def _():
        for j in range(PAIRS):
            for g in range(3):
                flat_s[pl.ds(3 * g + j, D, stride=9), :] = acc_s[j, :, g * LANES : (g + 1) * LANES]
        first_s[0:TAIL0, :] = flat_s[...].astype(BF16)
        first_s[TAIL0:KEPT, :] = tail_ref[0:16, :].astype(BF16)
        if first_s.shape[0] > KEPT:
            first_s[KEPT:, :] = jnp.zeros((first_s.shape[0] - KEPT, LANES), BF16)
        first = pltpu.make_async_copy(first_s, grads_ref.at[0], sems.at[0])
        first.start()
        tail_s[...] = tail_ref[16:80, :]
        sums = jnp.sum(sums_s[...], axis=1)
        heads = jnp.sum(heads_s[...], axis=1)
        heads = heads + pltpu.roll(heads, HD, 1)
        biases = jnp.sum(bias_s[...], axis=1)

        def put(row, value):
            tail_s[VEC_AT + row : VEC_AT + row + 1, :] = value

        for j in range(3):
            part = slice(j * LANES, (j + 1) * LANES)
            put(NORM_GAIN + j, sums[0:1, part])
            put(NORM_BIAS + j, sums[1:2, part])
            for g in range(3):
                put(QKV_BIAS + 3 * g + j, biases[j : j + 1, g * LANES : (g + 1) * LANES])
        put(QUERY, jnp.where(low_half(), heads[0:1], heads[1:2]))
        put(KEY, jnp.where(low_half(), heads[2:3], heads[3:4]))
        low_s[...] = tail_s[...].astype(BF16)
        last = pltpu.make_async_copy(low_s, grads_ref.at[3, TAIL3:KEPT], sems.at[1])
        last.start()
        first.wait()
        last.wait()


def attn_backward(x, resid, mixed, att, e, q, k, v, xq, xk, rq, rk, it, wp, vec, tail, grads):
    seqs, seq, _ = x.shape
    total = e.shape[-1]
    pair = pl.BlockSpec((1, 1, seq, LANES), lambda s, p: (s, p, 0, 0))
    whole = lambda *shape: pl.BlockSpec(shape, lambda s, p: (0,) * len(shape))
    full = pl.BlockSpec((1, seq, D), lambda s, p: (s, 0, 0))
    return pl.pallas_call(
        attn_backward_kernel,
        grid=(seqs, PAIRS),
        in_specs=[
            full,
            full,
            pl.BlockSpec((1, seq, LANES), lambda s, p: (s, 0, p)),
            pl.BlockSpec((1, seq, LANES), lambda s, p: (s, 0, p)),
            pl.BlockSpec((1, 1, 512, total), lambda s, p: (s, p, 0, 0)),
            pair,
            pair,
            pair,
            pair,
            pair,
            pair,
            pair,
            pair,
            whole(PAIRS, D, D),
            whole(*vec.shape),
            whole(80, LANES),
            pl.BlockSpec(memory_space=pl.ANY),
        ],
        out_shape=[
            jax.ShapeDtypeStruct((seqs, seq, D), BF16),
            jax.ShapeDtypeStruct(grads.shape, BF16),
        ],
        out_specs=[full, pl.BlockSpec(memory_space=pl.ANY)],
        input_output_aliases={16: 1},
        scratch_shapes=[
            pltpu.VMEM((seq, D), BF16),
            pltpu.VMEM((seq, D), F32),
            pltpu.VMEM((seq, LANES), F32),
            pltpu.VMEM((seq, LANES), F32),
            pltpu.VMEM((seq, LANES), F32),
            pltpu.VMEM((2, seq, LANES), BF16),
            pltpu.VMEM((seq, D), BF16),
            pltpu.VMEM((PAIRS, D, D), F32),
            pltpu.VMEM((QKV_ROWS, LANES), F32),
            pltpu.VMEM((2, 8, D), F32),
            pltpu.VMEM((4, 8, LANES), F32),
            pltpu.VMEM((PAIRS, 8, D), F32),
            pltpu.VMEM(grads.shape[1:], BF16),
            pltpu.VMEM((64, LANES), F32),
            pltpu.VMEM((64, LANES), BF16),
            pltpu.SemaphoreType.DMA((2,)),
        ],
        compiler_params=pltpu.CompilerParams(vmem_limit_bytes=VMEM),
        name="attn_backward",
    )(x, resid, mixed, att, e, q, k, v, xq, xk, rq, rk, it, wp, vec, tail, grads)


CHUNKS = 4


def padded_rows(n):
    unit = 16 * n * CHUNKS
    return -(-QUARTER // unit) * unit


def position():
    dp, shard = lax.axis_index("dp"), lax.axis_index("shard")
    return dp, shard, shard // 2, lax.rem(shard, 2), lax.rem(dp, 2)


def flip(dp, bit):
    return dp + (1 - 2 * lax.rem(dp // bit, 2)) * bit


def greet(peers):
    barrier = pltpu.get_barrier_semaphore()
    for peer in peers:
        pl.semaphore_signal(barrier, inc=1, device_id=peer, device_id_type=MESH)
    pl.semaphore_wait(barrier, len(peers))


class Spread:
    def __init__(self, own, out, sends, recvs, own_sem):
        dp, shard, y, core, x = position()
        self.own, self.out, self.sends, self.recvs, self.own_sem = own, out, sends, recvs, own_sem
        self.mine, self.across = shard, 2 * (1 - y) + core
        self.beside, self.diagonal = 2 * y + 1 - core, 2 * (1 - y) + 1 - core
        self.x = x
        self.core_peer, self.y_peer, self.x_peer = (dp, self.beside), (dp, self.across), (flip(dp, 1), shard)
        self.chunk = own.shape[0] // CHUNKS
        self.half = self.chunk // 2

    def rows(self, c, half=None):
        if half is None:
            return pl.ds(c * self.chunk, self.chunk)
        return pl.ds(pl.multiple_of(c * self.chunk + half * self.half, 16), self.half)

    def copy(self, c, kind, src, quarter, rows, peer):
        return pltpu.make_async_remote_copy(src_ref=src, dst_ref=self.out.at[quarter, rows], send_sem=self.sends.at[c, kind], recv_sem=self.recvs.at[c, kind], device_id=peer, device_id_type=MESH)

    def to_core(self, c):
        return self.copy(c, 0, self.own.at[self.rows(c)], self.mine, self.rows(c), self.core_peer)

    def to_y(self, c):
        rows = self.rows(c, self.x)
        return self.copy(c, 1, self.own.at[rows], self.mine, rows, self.y_peer)

    def onward(self, c, kind):
        rows = self.rows(c, 1 - self.x if kind == 4 else self.x)
        return self.copy(c, kind, self.out.at[self.across, rows], self.across, rows, self.x_peer if kind == 2 else self.core_peer)

    def start(self, c):
        self.to_y(c).start()
        self.to_core(c).start()
        rows = self.rows(c)
        pltpu.make_async_copy(self.own.at[rows], self.out.at[self.mine, rows], self.own_sem.at[c]).start()

    def middle(self, c):
        self.to_y(c).wait_recv()
        self.onward(c, 2).start()
        self.onward(c, 3).start()

    def end(self, c):
        self.onward(c, 2).wait_recv()
        self.onward(c, 4).start()

    def finish(self, c):
        rows = self.rows(c)
        pltpu.make_async_copy(self.own.at[rows], self.out.at[self.mine, rows], self.own_sem.at[c]).wait()
        self.to_y(c).wait_send()
        self.to_core(c).wait()
        self.onward(c, 2).wait_send()
        self.onward(c, 3).wait()
        self.onward(c, 4).wait()


def gather_kernel(master_ref, out_ref, own_s, sends, recvs, own_sem):
    dp, shard, y, core, x = position()
    spread = Spread(own_s, out_ref, sends, recvs, own_sem)
    greet([spread.core_peer, spread.y_peer, spread.x_peer])
    for c in range(CHUNKS):
        first, last = c * spread.chunk, (c + 1) * spread.chunk
        inside = max(min(last, QUARTER) - first, 0)
        if inside:
            own_s[first : first + inside, :] = master_ref[first : first + inside, :].astype(BF16)
        if first + inside < last:
            own_s[first + inside : last, :] = jnp.zeros((last - first - inside, LANES), BF16)
        spread.start(c)
    for c in range(CHUNKS + 1):
        if c < CHUNKS:
            spread.middle(c)
        if c > 0:
            spread.end(c - 1)
    for c in range(CHUNKS):
        spread.finish(c)


def gather_weights(master, padded):
    return pl.pallas_call(
        gather_kernel,
        in_specs=[pl.BlockSpec(memory_space=pltpu.VMEM)],
        out_shape=jax.ShapeDtypeStruct((4, padded, LANES), BF16),
        out_specs=pl.BlockSpec(memory_space=pl.ANY),
        scratch_shapes=[
            pltpu.VMEM((padded, LANES), BF16),
            pltpu.SemaphoreType.DMA((CHUNKS, 5)),
            pltpu.SemaphoreType.DMA((CHUNKS, 5)),
            pltpu.SemaphoreType.DMA((CHUNKS,)),
        ],
        compiler_params=pltpu.CompilerParams(collective_id=0, has_side_effects=True, vmem_limit_bytes=VMEM),
        name="gather_weights",
    )(master)


def adam(grad_sum, master, moment_one, moment_two, first_row):
    first = BETA_ONE * moment_one + (1.0 - BETA_ONE) * grad_sum
    second = BETA_TWO * moment_two + (1.0 - BETA_TWO) * grad_sum * grad_sum
    first_hat = first * (1.0 / (1.0 - BETA_ONE**STEP))
    second_hat = second * (1.0 / (1.0 - BETA_TWO**STEP))
    row = first_row + lax.broadcasted_iota(jnp.int32, grad_sum.shape, 0)
    decay = jnp.where(row < MAT_ROWS, DECAY, 0.0)
    return first, second, master - RATE * (first_hat / (jnp.sqrt(second_hat) + ADAM_EPS) + decay * master)


def reduce_kernel(n, scale, g_ref, master_ref, m1_ref, m2_ref, sum_ref, out_ref, vec_ref, pair_s, core_s, y_s, part_s, dp_s, all_s, new_s, vec_s, sends, recvs, loads, w_sends, w_recvs, own_sem, v_sends, v_recvs):
    dp, shard, y, core, x = position()
    bits = n.bit_length() - 1
    spread = Spread(new_s, out_ref, w_sends, w_recvs, own_sem)
    peers = [spread.core_peer, spread.y_peer] + [(flip(dp, 1 << b), shard) for b in range(bits)]
    chunk = part_s.shape[1]
    greet(peers)

    def remote(c, kind, src, dst, peer):
        return pltpu.make_async_remote_copy(src_ref=src, dst_ref=dst, send_sem=sends.at[c, kind], recv_sem=recvs.at[c, kind], device_id=peer, device_id_type=MESH)

    def load(c, j):
        return pltpu.make_async_copy(g_ref.at[2 * j + core, pl.ds(c * chunk, chunk)], pair_s.at[c, j], loads.at[c, j])

    def to_core(c, j):
        return remote(c, j, g_ref.at[2 * j + 1 - core, pl.ds(c * chunk, chunk)], core_s.at[c, j], peers[0])

    def to_y(c):
        return remote(c, 2, pair_s.at[c, 1 - y], y_s.at[c], peers[1])

    def mine(b):
        return lax.rem(dp // (1 << b), 2)

    def offset(b):
        return sum((mine(i) * (chunk >> (i + 1)) for i in range(b)), 0)

    def piece(b, half):
        size = chunk >> (b + 1)
        return pl.ds(pl.multiple_of(offset(b) + half * size, 16), size)

    def landing(b):
        return pl.ds(chunk - (chunk >> b), chunk >> (b + 1))

    def halve(c, b):
        return remote(c, 3 + b, part_s.at[c, piece(b, 1 - mine(b))], dp_s.at[c, landing(b)], peers[2 + b])

    def double(c, b):
        at = piece(b, mine(b))
        rows = pl.ds(pl.multiple_of(c * chunk + offset(b) + mine(b) * (chunk >> (b + 1)), 16), chunk >> (b + 1))
        return remote(c, 3 + bits + b, all_s.at[rows], all_s.at[rows], peers[2 + b])

    def add(a, b):
        return (a.astype(F32) + b.astype(F32)).astype(BF16)

    def stage(c, t):
        if t == 0:
            for j in range(2):
                load(c, j).wait()
                to_core(c, j).wait_recv()
                pair_s[c, j] = add(pair_s[c, j], core_s[c, j])
            to_y(c).start()
        elif t == 1:
            to_y(c).wait_recv()
            part_s[c] = add(pair_s[c, y], y_s[c])
            halve(c, 0).start()
        elif t < 2 + bits:
            b = t - 2
            halve(c, b).wait_recv()
            total = add(part_s[c, piece(b, mine(b)), :], dp_s[c, landing(b), :])
            if b + 1 < bits:
                part_s[c, piece(b, mine(b)), :] = total
                halve(c, b + 1).start()
            else:
                rows = pl.ds(pl.multiple_of(c * chunk + offset(bits), 16), chunk >> bits)
                all_s[rows, :] = total
                double(c, bits - 1).start()
        elif t < 2 + 2 * bits:
            b = bits - 1 - (t - 2 - bits)
            double(c, b).wait_recv()
            if b > 0:
                double(c, b - 1).start()
            else:
                update(c)
                spread.start(c)
        elif t == 2 + 2 * bits:
            spread.middle(c)
        elif t == 3 + 2 * bits:
            spread.end(c)

    def update(c):
        first, last = c * chunk, (c + 1) * chunk
        inside = max(min(last, QUARTER) - first, 0)
        if inside:
            rows = slice(first, first + inside)
            grad = all_s[rows, :].astype(F32) * scale
            new_s[rows, :] = adam(grad, master_ref[rows, :], m1_ref[rows, :], m2_ref[rows, :], shard * QUARTER + first)[2].astype(BF16)
        if first + inside < last:
            new_s[first + inside : last, :] = jnp.zeros((last - first - inside, LANES), BF16)

    for c in range(CHUNKS):
        for j in range(2):
            to_core(c, j).start()
            load(c, j).start()
    stages = 4 + 2 * bits
    for t in range(CHUNKS + stages - 1):
        for c in range(CHUNKS):
            if 0 <= t - c < stages:
                stage(c, t - c)

    def vectors(kind, quarter, peer):
        return pltpu.make_async_remote_copy(src_ref=vec_s.at[quarter], dst_ref=vec_s.at[quarter], send_sem=v_sends.at[kind], recv_sem=v_recvs.at[kind], device_id=peer, device_id_type=MESH)

    vec_s[spread.mine] = all_s[TAIL3:KEPT, :]
    vectors(0, spread.mine, spread.core_peer).start()
    vectors(1, spread.mine, spread.y_peer).start()
    vectors(1, spread.mine, spread.y_peer).wait_recv()
    vectors(2, spread.across, spread.core_peer).start()
    sum_ref[...] = all_s[...]
    for c in range(CHUNKS):
        for j in range(2):
            to_core(c, j).wait_send()
        to_y(c).wait_send()
        for b in range(bits):
            halve(c, b).wait_send()
            double(c, b).wait_send()
        spread.finish(c)
    vectors(0, spread.mine, spread.core_peer).wait()
    vectors(1, spread.mine, spread.y_peer).wait_send()
    vectors(2, spread.across, spread.core_peer).wait()
    vec_ref[...] = vec_s[3].astype(F32) * scale


def reduce_gradients(grads, master, moment_one, moment_two, n, sequences):
    padded = grads.shape[1]
    chunk = padded // CHUNKS
    bits = n.bit_length() - 1
    kinds = 3 + 2 * bits
    anywhere, vmem = pl.BlockSpec(memory_space=pl.ANY), pl.BlockSpec(memory_space=pltpu.VMEM)
    return pl.pallas_call(
        functools.partial(reduce_kernel, n, 1.0 / sequences),
        in_specs=[anywhere, vmem, vmem, vmem],
        out_shape=[
            jax.ShapeDtypeStruct((padded, LANES), BF16),
            jax.ShapeDtypeStruct((4, padded, LANES), BF16),
            jax.ShapeDtypeStruct((64, LANES), F32),
        ],
        out_specs=[vmem, anywhere, vmem],
        scratch_shapes=[
            pltpu.VMEM((CHUNKS, 2, chunk, LANES), BF16),
            pltpu.VMEM((CHUNKS, 2, chunk, LANES), BF16),
            pltpu.VMEM((CHUNKS, chunk, LANES), BF16),
            pltpu.VMEM((CHUNKS, chunk, LANES), BF16),
            pltpu.VMEM((CHUNKS, chunk, LANES), BF16),
            pltpu.VMEM((padded, LANES), BF16),
            pltpu.VMEM((padded, LANES), BF16),
            pltpu.VMEM((4, 64, LANES), BF16),
            pltpu.SemaphoreType.DMA((CHUNKS, kinds)),
            pltpu.SemaphoreType.DMA((CHUNKS, kinds)),
            pltpu.SemaphoreType.DMA((CHUNKS, 2)),
            pltpu.SemaphoreType.DMA((CHUNKS, 5)),
            pltpu.SemaphoreType.DMA((CHUNKS, 5)),
            pltpu.SemaphoreType.DMA((CHUNKS,)),
            pltpu.SemaphoreType.DMA((3,)),
            pltpu.SemaphoreType.DMA((3,)),
        ],
        compiler_params=pltpu.CompilerParams(collective_id=1, has_side_effects=True, vmem_limit_bytes=VMEM),
        name="reduce_gradients",
    )(grads, master, moment_one, moment_two)


UPDATE = 880


def finish_kernel(scale, sum_ref, master_ref, m1_ref, m2_ref, w_ref, next_ref, grad_ref, new_ref, first_ref, second_ref, copy_ref):
    b = pl.program_id(0)
    grad = sum_ref[...].astype(F32) * scale
    first, second, new = adam(grad, master_ref[...], m1_ref[...], m2_ref[...], lax.axis_index("shard") * QUARTER + b * UPDATE)
    grad_ref[...], first_ref[...], second_ref[...], new_ref[...] = grad, first, second, new
    for k in range(4):
        skip = k * (KEPT - QUARTER)

        @pl.when(b == k)
        def _():
            own = w_ref[0, :KEPT, :].astype(F32)
            if k == 3:
                copy_ref[...] = jnp.concatenate([own[skip:], own[:skip]], axis=0).astype(BF16)
            else:
                after = next_ref[0].astype(F32)
                copy_ref[...] = jnp.concatenate([own[skip:QUARTER], after[: skip + KEPT - QUARTER]], axis=0).astype(BF16)


def finish(sums, master, moment_one, moment_two, weights, sequences):
    rows = lambda dtype: pl.BlockSpec((UPDATE, LANES), lambda b: (b, 0))
    f32 = jax.ShapeDtypeStruct((QUARTER, LANES), F32)
    padded = weights.shape[1]
    return pl.pallas_call(
        functools.partial(finish_kernel, 1.0 / sequences),
        grid=(4,),
        in_specs=[rows(BF16), rows(F32), rows(F32), rows(F32), pl.BlockSpec((1, padded, LANES), lambda b: (b, 0, 0)), pl.BlockSpec((1, 32, LANES), lambda b: (jnp.minimum(b + 1, 3), 0, 0))],
        out_shape=[f32, f32, f32, f32, jax.ShapeDtypeStruct((ALL_ROWS, LANES), BF16)],
        out_specs=[rows(F32), rows(F32), rows(F32), rows(F32), pl.BlockSpec((KEPT, LANES), lambda b: (b, 0))],
        compiler_params=pltpu.CompilerParams(vmem_limit_bytes=VMEM),
        name="finish",
    )(sums, master, moment_one, moment_two, weights, weights)


def shards(patches, segments, out_grad, master, moment_one, moment_two):
    seqs, seq, _ = patches.shape
    n = lax.axis_size("dp")
    sequences = seqs * n * lax.axis_size("shard")
    rows = lambda a: a.reshape(QUARTER, LANES)
    master, moment_one, moment_two = rows(master), rows(moment_one), rows(moment_two)
    weights = gather_weights(master, padded_rows(n))
    vec = weights[3, TAIL3:KEPT]
    slot = jnp.arange(LANES, dtype=jnp.int32) % HD
    same = segments[:, :, None] == slot
    qf = jnp.where((slot < 8) & ~same, 1.0, 0.0).astype(BF16)
    kf = jnp.where((slot < 8) & same, FAR, 0.0).astype(BF16)
    att, e, q, k, v, xq, xk, rq, rk, it, wp = attn_forward(patches, qf, kf, weights, vec)
    flat = lambda a: a.reshape(seqs * seq, D)
    act, mixed, resid, grads, tail = mlp(flat(patches), flat(att), flat(out_grad), weights, vec)
    whole = lambda a: a.reshape(seqs, seq, D)
    input_grad, grads = attn_backward(patches, whole(resid), whole(mixed), att, e, q, k, v, xq, xk, rq, rk, it, wp, vec, tail, grads)
    sums, weights, vectors = reduce_gradients(grads, master, moment_one, moment_two, n, sequences)
    vector_grad = vectors[VEC_AT : VEC_AT + ALL_ROWS - MAT_ROWS].reshape(-1)
    updated = finish(sums, master, moment_one, moment_two, weights, sequences)
    grad_sum, new_master, first_moment, second_moment, weights_copy = [a.reshape(-1) for a in updated]
    return whole(act), input_grad, grad_sum, vector_grad, new_master, first_moment, second_moment, weights_copy


def solution(mesh):
    split_rows = P(("dp", "shard"), None, None)
    return jax.shard_map(
        shards,
        mesh=mesh,
        in_specs=(split_rows, P(("dp", "shard"), None), split_rows, P("shard"), P("shard"), P("shard")),
        out_specs=(split_rows, split_rows, P("shard"), P(), P("shard"), P("shard"), P("shard"), P()),
        check_vma=False,
    )
```

```python
import functools

import jax
import jax.numpy as jnp
from jax import lax
from jax.experimental import pallas as pl
from jax.experimental.pallas import tpu as pltpu
from jax.sharding import PartitionSpec as P

F32, BF16 = jnp.float32, jnp.bfloat16
MESH = pl.DeviceIdType.MESH
D, HEADS, HD, FF = 384, 6, 64, 1536
STEP = 3
PARAMS = 1775104
EPS = 1e-06
FAR = -1e30
BETA_ONE, BETA_TWO, RATE, DECAY, ADAM_EPS = 0.5, 0.5, 0.03, 0.1, 1e-08

LANES = 128
PAIRS = HEADS // 2
QKV_ROWS = 3 * D * D // LANES
OUT_ROWS = D * D // LANES
UP_ROWS = D * FF // LANES
MAT_ROWS = QKV_ROWS + OUT_ROWS + 2 * UP_ROWS
ALL_ROWS = PARAMS // LANES
QUARTER = ALL_ROWS // 4
KEPT = -(-QUARTER // 16) * 16
TAIL0 = QKV_ROWS
TAIL3 = 3408
VEC_AT = MAT_ROWS - 3 * QUARTER - TAIL3
NORM_GAIN, NORM_BIAS, QKV_BIAS, QUERY, KEY, OUT_BIAS, MLP_GAIN, MLP_BIAS, UP_BIAS, DOWN_BIAS = 0, 3, 6, 15, 16, 17, 20, 23, 26, 38
VMEM = 60 * 2**20


def dot(a, b):
    return jnp.dot(a, b, preferred_element_type=F32)


def dot_nt(a, b):
    return lax.dot_general(a, b, (((1,), (1,)), ((), ())), preferred_element_type=F32)


def dot_tn(a, b):
    return lax.dot_general(a, b, (((0,), (0,)), ((), ())), preferred_element_type=F32)


def row_of(vec, first, count):
    rows = [vec[VEC_AT + first + j : VEC_AT + first + j + 1, :] for j in range(count)]
    return jnp.concatenate(rows, axis=1) if count > 1 else rows[0]


def low_half(rows=1):
    return lax.broadcasted_iota(jnp.int32, (rows, LANES), 1) < HD


def both_halves(row, half):
    other = pltpu.roll(row, HD, 1)
    return jnp.where(low_half(), row, other) if half == 0 else jnp.where(low_half(), other, row)


def group_matrix(value, swapped=False):
    r = lax.rem(lax.broadcasted_iota(jnp.int32, (2 * LANES, LANES), 0), LANES) // HD
    c = lax.broadcasted_iota(jnp.int32, (2 * LANES, LANES), 1) // HD
    hit = (r != c) if swapped else (r == c)
    return jnp.where(hit, value, 0.0).astype(BF16)


def split(v):
    high = v.astype(BF16)
    return jnp.concatenate([high, (v - high.astype(F32)).astype(BF16)], axis=1)


def window(i, count):
    first, last = max(i - 1, 0), min(i + 2, count)
    return 256 * first, 256 * (last - first)


def columns(i, count):
    return sum(window(j, count)[1] for j in range(i))


def norm_stats(v):
    mean = jnp.mean(v, axis=1, keepdims=True)
    c = v - mean
    var = jnp.mean(c * c, axis=1, keepdims=True)
    r = lax.rsqrt(var + EPS)
    return c * r, r


def attn_forward_kernel(x_ref, seg_ref, w_ref, vec_ref, att_ref, e_ref, q_ref, k_ref, v_ref, xq_ref, xk_ref, rq_ref, rk_ref, it_ref, wp_ref, n_s, wf_s, ka_s, va_s, qf_s, kf_s):
    s, p = pl.program_id(0), pl.program_id(1)
    seq = x_ref.shape[1]
    blocks = seq // 256

    @pl.when((s == 0) & (p == 0))
    def _():
        wf_s[...] = w_ref[0, :QKV_ROWS].astype(F32)
        for j in range(PAIRS):
            for g in range(3):
                wp_ref[:, j * D + g * LANES : j * D + (g + 1) * LANES] = wf_s[pl.ds(3 * g + j, D, stride=9), :].astype(BF16)

    @pl.when(p == 0)
    def _():
        gain = row_of(vec_ref[...].astype(F32), NORM_GAIN, 3)
        bias = row_of(vec_ref[...].astype(F32), NORM_BIAS, 3)

        def body(i, carry):
            rows = pl.ds(pl.multiple_of(i * 256, 256), 256)
            xhat, _ = norm_stats(x_ref[0, rows, :].astype(F32))
            n_s[rows, :] = (xhat * gain + bias).astype(BF16)
            return carry

        lax.fori_loop(0, blocks, body, 0, unroll=True)
        slot = lax.broadcasted_iota(jnp.int32, (16, seq), 0)
        hit = jnp.where(seg_ref[pl.ds(s, 1), :] == slot, 1.0, 0.0)
        lane = lax.rem(lax.broadcasted_iota(jnp.int32, (16, LANES), 1), HD)
        place = (lane == lax.broadcasted_iota(jnp.int32, (16, LANES), 0)) & (lane < 8)
        qf_s[...] = dot_tn((1.0 - hit).astype(BF16), jnp.where(place, 1.0, 0.0).astype(BF16)).astype(BF16)
        kf_s[...] = dot_tn(hit.astype(BF16), jnp.where(place, FAR, 0.0).astype(BF16)).astype(BF16)

    vec = vec_ref[...].astype(F32)
    qkv = vec[VEC_AT + QKV_BIAS : VEC_AT + QKV_BIAS + 9, :]
    which = lax.broadcasted_iota(jnp.int32, (9, LANES), 0)
    pick = lambda g: jnp.sum(jnp.where(which == 3 * g + p, qkv, 0.0), axis=0, keepdims=True)
    bias = jnp.concatenate([pick(0), pick(1), pick(2)], axis=1)
    qrow, krow = row_of(vec, QUERY, 1), row_of(vec, KEY, 1)
    qg, qb = both_halves(qrow, 0), both_halves(qrow, 1)
    kg, kb = both_halves(krow, 0), both_halves(krow, 1)
    means = group_matrix(1.0 / HD)
    w = wp_ref[:, pl.ds(pl.multiple_of(p * D, D), D)]

    def project(i, carry):
        rows = pl.ds(pl.multiple_of(i * 256, 256), 256)
        low = low_half(256)
        pr = dot(n_s[rows, :], w) + bias

        def head_norm(v):
            c = v - dot(split(v), means)
            r = lax.rsqrt(dot(split(c * c), means) + EPS)
            return c * r, r

        xq, rq = head_norm(pr[:, :LANES])
        xk, rk = head_norm(pr[:, LANES : 2 * LANES])
        q_ref[0, 0, rows, :] = ((xq * qg + qb) * HD**-0.5).astype(BF16)
        k = xk * kg + kb
        v = pr[:, 2 * LANES :]
        k_ref[0, 0, rows, :] = k.astype(BF16)
        v_ref[0, 0, rows, :] = v.astype(BF16)
        kf = kf_s[rows, :].astype(F32)
        ka_s[0, rows, :] = jnp.where(low, k, kf).astype(BF16)
        ka_s[1, rows, :] = jnp.where(low, kf, k).astype(BF16)
        va_s[0, rows, :] = jnp.where(low, v, 1.0).astype(BF16)
        va_s[1, rows, :] = jnp.where(low, 1.0, v).astype(BF16)
        xq_ref[0, 0, rows, :] = xq.astype(BF16)
        xk_ref[0, 0, rows, :] = xk.astype(BF16)
        rq_ref[0, 0, rows, :] = rq
        rk_ref[0, 0, rows, :] = rk
        return carry

    lax.fori_loop(0, blocks, project, 0, unroll=True)

    low = low_half(256)
    for i in range(blocks):
        start, width = window(i, blocks)
        at = columns(i, blocks)
        rows = slice(256 * i, 256 * (i + 1))
        q = q_ref[0, 0, rows, :].astype(F32)
        qf = qf_s[rows, :].astype(F32)
        sums = []
        for h in range(2):
            qa = (jnp.where(low, q, qf) if h == 0 else jnp.where(low, qf, q)).astype(BF16)
            scores = dot_nt(qa, ka_s[h, start : start + width, :])
            e = jnp.exp(scores - jnp.max(scores, axis=1, keepdims=True)).astype(BF16)
            e_ref[0, 0, 256 * h : 256 * (h + 1), at : at + width] = e
            sums.append(dot(e, va_s[h, start : start + width, :]))
        mixed = jnp.where(low, sums[0], sums[1])
        inverse = 1.0 / pltpu.roll(jnp.where(low, sums[1], sums[0]), HD, 1)
        att_ref[0, rows, :] = (mixed * inverse).astype(BF16)
        it_ref[0, 0, rows, :] = inverse


def attn_forward(x, segments, weights, vec):
    seqs, seq, _ = x.shape
    total = columns(seq // 256, seq // 256)
    pair = lambda dtype: (jax.ShapeDtypeStruct((seqs, PAIRS, seq, LANES), dtype), pl.BlockSpec((1, 1, seq, LANES), lambda s, p: (s, p, 0, 0)))
    outs = [
        (jax.ShapeDtypeStruct((seqs, seq, D), BF16), pl.BlockSpec((1, seq, LANES), lambda s, p: (s, 0, p))),
        (jax.ShapeDtypeStruct((seqs, PAIRS, 512, total), BF16), pl.BlockSpec((1, 1, 512, total), lambda s, p: (s, p, 0, 0))),
        pair(BF16),
        pair(BF16),
        pair(BF16),
        pair(BF16),
        pair(BF16),
        pair(F32),
        pair(F32),
        pair(F32),
        (jax.ShapeDtypeStruct((D, 3 * D), BF16), pl.BlockSpec((D, 3 * D), lambda s, p: (0, 0))),
    ]
    return pl.pallas_call(
        attn_forward_kernel,
        grid=(seqs, PAIRS),
        in_specs=[
            pl.BlockSpec((1, seq, D), lambda s, p: (s, 0, 0)),
            pl.BlockSpec(segments.shape, lambda s, p: (0, 0)),
            pl.BlockSpec((1, QKV_ROWS, LANES), lambda s, p: (0, 0, 0)),
            pl.BlockSpec(vec.shape, lambda s, p: (0, 0)),
        ],
        out_shape=[o[0] for o in outs],
        out_specs=[o[1] for o in outs],
        scratch_shapes=[
            pltpu.VMEM((seq, D), BF16),
            pltpu.VMEM((QKV_ROWS, LANES), F32),
            pltpu.VMEM((2, seq, LANES), BF16),
            pltpu.VMEM((2, seq, LANES), BF16),
            pltpu.VMEM((seq, LANES), BF16),
            pltpu.VMEM((seq, LANES), BF16),
        ],
        compiler_params=pltpu.CompilerParams(vmem_limit_bytes=VMEM),
        name="attn_forward",
    )(x, segments, weights, vec)


def gelu_parts(x):
    bell = jnp.exp(x * x * -0.5)
    d = 1.0 + (0.3275911 * 0.5**0.5) * jnp.abs(x)
    t = pl.reciprocal(d, approx=True)
    t = t * (2.0 - d * t)
    poly = t * (0.127414796 + t * (-0.142248368 + t * (0.7107068705 + t * (-0.7265760135 + t * 0.5307027145))))
    tail = poly * bell
    share = jnp.where(x >= 0, 1.0 - tail, tail)
    return x * share, share + x * bell * 0.3989422804014327


def mlp_kernel(x_ref, att_ref, og_ref, w_ref, vec_ref, act_ref, mixed_ref, branch_ref, grads_ref, tail_ref, flat_s, wout_s, wup_s, wdown_s, mid_s, hid_s, pre_s, branch_s, colsum_s, upsum_s):
    t = pl.program_id(0)
    up_at, down_at = OUT_ROWS, OUT_ROWS + UP_ROWS
    step = KEPT // 7
    vec = vec_ref[...].astype(F32)
    tile = x_ref.shape[0]

    @pl.when(t == 0)
    def _():
        flat_s[0:16, :] = w_ref[0, TAIL0:KEPT].astype(F32)
        for k in range(1, 4):
            for c in range(7):
                at = k * QUARTER - QKV_ROWS + c * step
                count = min(step, flat_s.shape[0] - at)
                flat_s[at : at + count, :] = w_ref[k, c * step : (c + 1) * step].astype(F32)[:count]
        for j in range(3):
            wout_s[:, j * LANES : (j + 1) * LANES] = flat_s[pl.ds(j, D, stride=3), :].astype(BF16)
            wdown_s[:, j * LANES : (j + 1) * LANES] = flat_s[pl.ds(down_at + j, FF, stride=3), :].astype(BF16)
        for j in range(12):
            wup_s[:, j * LANES : (j + 1) * LANES] = flat_s[pl.ds(up_at + j, D, stride=12), :].astype(BF16)
        colsum_s[...] = jnp.zeros_like(colsum_s)
        upsum_s[...] = jnp.zeros_like(upsum_s)

    rows = pl.ds(pl.multiple_of(t * tile, tile), tile)
    fold = lambda v: jnp.sum(v.reshape(tile // 8, 8, v.shape[1]), axis=0)
    og = og_ref[rows, :]
    att = att_ref[rows, :]
    og_f = og.astype(F32)
    residual = x_ref[...].astype(F32) + dot(att, wout_s[...]) + row_of(vec, OUT_BIAS, 3)
    xhat, r = norm_stats(residual)
    gain = row_of(vec, MLP_GAIN, 3)
    mid = (xhat * gain + row_of(vec, MLP_BIAS, 3)).astype(BF16)
    mid_s[rows, :] = mid
    act = residual + row_of(vec, DOWN_BIAS, 3)
    mid_grad = jnp.zeros((tile, D), F32)
    wide = 512
    for c in range(FF // wide):
        cols = slice(c * wide, (c + 1) * wide)
        pre = dot(mid, wup_s[:, cols]) + row_of(vec, UP_BIAS + c * wide // LANES, wide // LANES)
        act_grad = dot_nt(og, wdown_s[cols, :])
        hidden, slope = gelu_parts(pre)
        hidden = hidden.astype(BF16)
        pre_grad = (act_grad * slope).astype(BF16)
        hid_s[rows, cols] = hidden
        pre_s[rows, cols] = pre_grad
        upsum_s[:, cols] += fold(pre_grad.astype(F32))
        act = act + dot(hidden, wdown_s[cols, :])
        mid_grad = mid_grad + dot_nt(pre_grad, wup_s[:, cols])
    act_ref[...] = act.astype(BF16)
    e_hat = mid_grad * gain
    resid = og_f + (e_hat - jnp.mean(e_hat, axis=1, keepdims=True) - xhat * jnp.mean(e_hat * xhat, axis=1, keepdims=True)) * r
    branch = resid.astype(BF16)
    branch_ref[...] = branch
    branch_s[rows, :] = branch
    mixed_ref[...] = dot_nt(branch, wout_s[...]).astype(BF16)
    colsum_s[0] += fold(og_f)
    colsum_s[1] += fold(mid_grad * xhat)
    colsum_s[2] += fold(mid_grad)
    colsum_s[3] += fold(branch.astype(F32))

    @pl.when(t == pl.num_programs(0) - 1)
    def _():
        for j in range(3):
            flat_s[pl.ds(j, D, stride=3), :] = dot_tn(att_ref[...], branch_s[:, j * LANES : (j + 1) * LANES])

        def ups(c, carry):
            g = dot_tn(mid_s[...], pre_s[:, pl.ds(pl.multiple_of(c * 256, 256), 256)])
            for j in range(2):
                flat_s[pl.ds(up_at + 2 * c + j, D, stride=12), :] = g[:, j * LANES : (j + 1) * LANES]
            return carry

        lax.fori_loop(0, FF // 256, ups, 0, unroll=True)

        def downs(c, carry):
            g = dot_tn(hid_s[:, pl.ds(pl.multiple_of(c * 256, 256), 256)], og_ref[...])
            for j in range(3):
                flat_s[pl.ds(down_at + 768 * c + j, 256, stride=3), :] = g[:, j * LANES : (j + 1) * LANES]
            return carry

        lax.fori_loop(0, FF // 256, downs, 0, unroll=True)
        sums = jnp.sum(colsum_s[...], axis=1)
        upsum = jnp.sum(upsum_s[...], axis=0, keepdims=True)
        vec_at = MAT_ROWS - QKV_ROWS
        flat_s[vec_at:, :] = jnp.zeros((flat_s.shape[0] - vec_at, LANES), F32)
        for j in range(3):
            part = slice(j * LANES, (j + 1) * LANES)
            flat_s[vec_at + DOWN_BIAS + j : vec_at + DOWN_BIAS + j + 1, :] = sums[0:1, part]
            flat_s[vec_at + MLP_GAIN + j : vec_at + MLP_GAIN + j + 1, :] = sums[1:2, part]
            flat_s[vec_at + MLP_BIAS + j : vec_at + MLP_BIAS + j + 1, :] = sums[2:3, part]
            flat_s[vec_at + OUT_BIAS + j : vec_at + OUT_BIAS + j + 1, :] = sums[3:4, part]
        for j in range(12):
            flat_s[vec_at + UP_BIAS + j : vec_at + UP_BIAS + j + 1, :] = upsum[:, j * LANES : (j + 1) * LANES]
        grads_ref[0] = jnp.zeros(grads_ref.shape[1:], BF16)
        for k in range(1, 4):
            for c in range(7):
                at = k * QUARTER - QKV_ROWS + c * step
                grads_ref[k, c * step : (c + 1) * step, :] = flat_s[at : at + step, :].astype(BF16)
            if grads_ref.shape[1] > KEPT:
                grads_ref[k, KEPT:, :] = jnp.zeros((grads_ref.shape[1] - KEPT, LANES), BF16)
        tail_ref[0:16, :] = flat_s[0:16, :]
        tail_ref[16:80, :] = flat_s[3 * QUARTER - QKV_ROWS + TAIL3 : 3 * QUARTER - QKV_ROWS + KEPT, :]


def mlp(x, att, og, weights, vec):
    tokens = x.shape[0]
    tile = 512
    padded = 3 * QUARTER + KEPT - QKV_ROWS
    tiled = pl.BlockSpec((tile, D), lambda t: (t, 0))
    whole = lambda *shape: pl.BlockSpec(shape, lambda t: (0,) * len(shape))
    return pl.pallas_call(
        mlp_kernel,
        grid=(tokens // tile,),
        in_specs=[tiled, whole(tokens, D), whole(tokens, D), whole(*weights.shape), whole(*vec.shape)],
        out_shape=[
            jax.ShapeDtypeStruct((tokens, D), BF16),
            jax.ShapeDtypeStruct((tokens, D), BF16),
            jax.ShapeDtypeStruct((tokens, D), BF16),
            jax.ShapeDtypeStruct(weights.shape, BF16),
            jax.ShapeDtypeStruct((80, LANES), F32),
        ],
        out_specs=[tiled, tiled, tiled, whole(*weights.shape), whole(80, LANES)],
        scratch_shapes=[
            pltpu.VMEM((padded, LANES), F32),
            pltpu.VMEM((D, D), BF16),
            pltpu.VMEM((D, FF), BF16),
            pltpu.VMEM((FF, D), BF16),
            pltpu.VMEM((tokens, D), BF16),
            pltpu.VMEM((tokens, FF), BF16),
            pltpu.VMEM((tokens, FF), BF16),
            pltpu.VMEM((tokens, D), BF16),
            pltpu.VMEM((4, 8, D), F32),
            pltpu.VMEM((8, FF), F32),
        ],
        compiler_params=pltpu.CompilerParams(vmem_limit_bytes=VMEM),
        name="mlp",
    )(x, att, og, weights, vec)


CHUNKS = 4
STEPS = 5


def whole_rows(rows, n, parts):
    unit = 16 * n * parts
    return -(-rows // unit) * unit


def position():
    dp, shard = lax.axis_index("dp"), lax.axis_index("shard")
    return dp, shard, shard // 2, lax.rem(shard, 2), lax.rem(dp, 2)


def flip(dp, bit):
    return dp + (1 - 2 * lax.rem(dp // bit, 2)) * bit


class Peers:
    def __init__(self, n):
        self.dp, self.shard, self.y, self.core, self.x = position()
        self.beside, self.across = 2 * self.y + 1 - self.core, 2 * (1 - self.y) + self.core
        self.core_peer, self.y_peer = (self.dp, self.beside), (self.dp, self.across)
        self.n = n
        self.x_peer = (flip(self.dp, 1), self.shard)
        self.line, self.lines = self.dp // 2, n // 2

    def dp_peer(self, k):
        return (lax.rem(self.dp + k, self.n), self.shard)

    def line_peer(self, k):
        return (lax.rem(self.line + k, self.lines) * 2 + self.x, self.shard)

    def group_peer(self, k):
        return (self.dp, lax.rem(self.shard + k, 4))

    def greet(self, peers):
        barrier = pltpu.get_barrier_semaphore()
        for peer in peers:
            pl.semaphore_signal(barrier, inc=1, device_id=peer, device_id_type=MESH)
        pl.semaphore_wait(barrier, len(peers))


def remote(src, dst, send, recv, peer):
    return pltpu.make_async_remote_copy(src_ref=src, dst_ref=dst, send_sem=send, recv_sem=recv, device_id=peer, device_id_type=MESH)


def add(a, b):
    return (a.astype(F32) + b.astype(F32)).astype(BF16)


class Reduction:
    stages = 6

    def __init__(self, at, source, loads, pair, core, y, part, land, lands, total, sends, recvs):
        self.at, self.source, self.loads = at, source, loads
        self.pair, self.core, self.y, self.part, self.land, self.lands, self.total = pair, core, y, part, land, lands, total
        self.sends, self.recvs = sends, recvs
        self.half = part.shape[0] // 2
        self.size = self.half // at.lines

    def remote(self, kind, src, dst, peer):
        return remote(src, dst, self.sends.at[kind], self.recvs.at[kind], peer)

    def to_core(self, j):
        return self.remote(j, self.source(2 * j + 1 - self.at.core), self.core.at[j], self.at.core_peer)

    def load(self, j):
        return pltpu.make_async_copy(self.source(2 * j + self.at.core), self.pair.at[j], self.loads.at[j])

    def to_y(self):
        return self.remote(2, self.pair.at[1 - self.at.y], self.y, self.at.y_peer)

    def half_of(self, x):
        return pl.ds(pl.multiple_of(x * self.half, 16), self.half)

    def piece(self, line):
        return pl.ds(pl.multiple_of(self.at.x * self.half + line * self.size, 16), self.size)

    def to_x(self):
        return self.remote(3, self.part.at[self.half_of(1 - self.at.x)], self.land, self.at.x_peer)

    def back_x(self):
        rows = self.half_of(self.at.x)
        return self.remote(4, self.total.at[rows], self.total.at[rows], self.at.x_peer)

    def to_line(self, k):
        return self.remote(4 + k, self.part.at[self.piece(lax.rem(self.at.line + k, self.at.lines))], self.lands.at[k], self.at.line_peer(k))

    def back_line(self, k):
        rows = self.piece(self.at.line)
        return self.remote(3 + self.at.lines + k, self.total.at[rows], self.total.at[rows], self.at.line_peer(k))

    def begin(self):
        for j in range(2):
            self.to_core(j).start()
            self.load(j).start()

    def stage(self, t):
        others = range(1, self.at.lines)
        if t == 0:
            for j in range(2):
                self.load(j).wait()
                self.to_core(j).wait_recv()
                self.pair[j] = add(self.pair[j], self.core[j])
            self.to_y().start()
        elif t == 1:
            self.to_y().wait_recv()
            self.part[...] = add(self.pair[self.at.y], self.y[...])
            self.to_x().start()
        elif t == 2:
            self.to_x().wait_recv()
            rows = self.half_of(self.at.x)
            self.part[rows, :] = add(self.part[rows, :], self.land[...])
            for k in others:
                self.to_line(k).start()
        elif t == 3:
            rows = self.piece(self.at.line)
            total = self.part[rows, :].astype(F32)
            for k in others:
                self.to_line(k).wait_recv()
                total = total + self.lands[k].astype(F32)
            self.total[rows, :] = total.astype(BF16)
            for k in others:
                self.back_line(k).start()
        elif t == 4:
            for k in others:
                self.back_line(k).wait_recv()
            self.back_x().start()
        else:
            self.back_x().wait_recv()

    def finish(self):
        for j in range(2):
            self.to_core(j).wait_send()
        self.to_y().wait_send()
        self.to_x().wait_send()
        self.back_x().wait_send()
        for k in range(1, self.at.lines):
            self.to_line(k).wait_send()
            self.back_line(k).wait_send()


class Late:
    def __init__(self, at, blocks, lands, part, pieces, out, update, sends, recvs):
        self.at, self.blocks, self.lands, self.part, self.pieces, self.out, self.update = at, blocks, lands, part, pieces, out, update
        self.sends, self.recvs = sends, recvs
        self.size = part.shape[0] // at.n

    def remote(self, kind, src, dst, peer):
        return remote(src, dst, self.sends.at[kind], self.recvs.at[kind], peer)

    def rows(self, d):
        return pl.ds(pl.multiple_of(d * self.size, 16), self.size)

    def group(self, k):
        return self.remote(k - 1, self.blocks.at[lax.rem(self.at.shard + k, 4)], self.lands.at[k - 1], self.at.group_peer(k))

    def pieces_out(self, k):
        return self.remote(5 + k, self.part.at[self.rows(lax.rem(self.at.dp + k, self.at.n))], self.pieces.at[k], self.at.dp_peer(k))

    def pieces_back(self, k):
        mine = self.out.at[:, self.at.shard, self.rows(self.at.dp)]
        return self.remote(4 + self.at.n + k, mine, mine, self.at.dp_peer(k))

    def weights(self, k):
        mine = self.out.at[1, self.at.shard]
        return self.remote(2 + k, mine, mine, self.at.group_peer(k))

    def sums(self, place):
        mine = self.out.at[0, place]
        return self.remote(3 + 2 * self.at.n + place, mine, mine, (self.at.dp, 0))

    def begin(self):
        for k in (2, 3, 1):
            self.group(k).start()

    def stage(self, t):
        others = range(1, self.at.n)
        if t == 0:
            total = self.blocks[self.at.shard].astype(F32)
            for k in (1, 2, 3):
                self.group(k).wait_recv()
                total = total + self.lands[k - 1].astype(F32)
            self.part[...] = total.astype(BF16)
            for k in others:
                self.pieces_out(k).start()
        elif t == 1:
            total = self.part[self.rows(self.at.dp), :].astype(F32)
            for k in others:
                self.pieces_out(k).wait_recv()
                total = total + self.pieces[k].astype(F32)
            low = total.astype(BF16)
            self.out[0, self.at.shard, self.rows(self.at.dp), :] = low
            self.out[1, self.at.shard, self.rows(self.at.dp), :] = self.update(low.astype(F32)).astype(BF16)
            for k in others:
                self.pieces_back(k).start()
        elif t == 2:
            for k in others:
                self.pieces_back(k).wait_recv()
            for place in (1, 2):

                @pl.when(self.at.shard == place)
                def _():
                    self.sums(place).start()

            for k in (2, 3, 1):
                self.weights(k).start()
        else:
            for k in (1, 2, 3):
                self.weights(k).wait_recv()

            @pl.when(self.at.shard == 0)
            def _():
                for place in (1, 2):
                    self.sums(place).wait_recv()

    def finish(self):
        for k in (1, 2, 3):
            self.group(k).wait_send()
            self.weights(k).wait_send()
        for k in range(1, self.at.n):
            self.pieces_out(k).wait_send()
            self.pieces_back(k).wait_send()
        for place in (1, 2):

            @pl.when(self.at.shard == place)
            def _():
                self.sums(place).wait_send()


class Total:
    def __init__(self, at, groups, all_dp, out, sends, recvs):
        self.at, self.groups, self.all_dp, self.out, self.sends, self.recvs = at, groups, all_dp, out, sends, recvs

    def group(self, k):
        mine = self.groups.at[self.at.shard]
        return remote(mine, mine, self.sends.at[k - 1], self.recvs.at[k - 1], self.at.group_peer(k))

    def far(self, k):
        mine = self.all_dp.at[self.at.dp]
        return remote(mine, mine, self.sends.at[2 + k], self.recvs.at[2 + k], self.at.dp_peer(k))

    def begin(self):
        for k in (2, 3, 1):
            self.group(k).start()

    def middle(self):
        for k in (1, 2, 3):
            self.group(k).wait_recv()
        self.all_dp[self.at.dp] = (self.groups[0] + self.groups[1]) + (self.groups[2] + self.groups[3])
        for k in range(1, self.at.n):
            self.far(k).start()

    def end(self):
        for k in range(1, self.at.n):
            self.far(k).wait_recv()
        total = self.all_dp[0]
        for k in range(1, self.at.n):
            total = total + self.all_dp[k]
        self.out[...] = total

    def finish(self):
        for k in (1, 2, 3):
            self.group(k).wait_send()
        for k in range(1, self.at.n):
            self.far(k).wait_send()


class Share:
    def __init__(self, at, buf, sends, recvs):
        self.at, self.buf, self.sends, self.recvs = at, buf, sends, recvs

    def copy(self, kind):
        part = self.buf.at[self.at.across if kind == 2 else self.at.shard]
        return remote(part, part, self.sends.at[kind], self.recvs.at[kind], self.at.y_peer if kind == 1 else self.at.core_peer)

    def start(self):
        self.copy(1).start()
        self.copy(0).start()

    def middle(self):
        self.copy(1).wait_recv()
        self.copy(2).start()

    def end(self):
        self.copy(0).wait_recv()
        self.copy(2).wait_recv()

    def finish(self):
        for kind in range(3):
            self.copy(kind).wait_send()


class Spread:
    def __init__(self, at, own, out, chunks, sends, recvs, own_sem):
        self.at, self.own, self.out, self.sends, self.recvs, self.own_sem = at, own, out, sends, recvs, own_sem
        self.chunk = own.shape[0] // chunks
        self.half = self.chunk // 2

    def rows(self, c, half=None):
        if half is None:
            return pl.ds(c * self.chunk, self.chunk)
        return pl.ds(pl.multiple_of(c * self.chunk + half * self.half, 16), self.half)

    def copy(self, c, kind, src, quarter, rows, peer):
        return remote(src, self.out.at[quarter, rows], self.sends.at[c, kind], self.recvs.at[c, kind], peer)

    def to_core(self, c):
        return self.copy(c, 0, self.own.at[self.rows(c)], self.at.shard, self.rows(c), self.at.core_peer)

    def to_y(self, c):
        rows = self.rows(c, self.at.x)
        return self.copy(c, 1, self.own.at[rows], self.at.shard, rows, self.at.y_peer)

    def onward(self, c, kind):
        rows = self.rows(c, 1 - self.at.x if kind == 4 else self.at.x)
        return self.copy(c, kind, self.out.at[self.at.across, rows], self.at.across, rows, self.at.x_peer if kind == 2 else self.at.core_peer)

    def keep(self, c):
        rows = self.rows(c)
        return pltpu.make_async_copy(self.own.at[rows], self.out.at[self.at.shard, rows], self.own_sem.at[c])

    def start(self, c):
        self.to_y(c).start()
        self.to_core(c).start()
        self.keep(c).start()

    def middle(self, c):
        self.to_y(c).wait_recv()
        self.onward(c, 2).start()
        self.onward(c, 3).start()

    def end(self, c):
        self.onward(c, 2).wait_recv()
        self.onward(c, 4).start()

    def finish(self, c):
        self.keep(c).wait()
        self.to_y(c).wait_send()
        self.to_core(c).wait()
        self.onward(c, 2).wait_send()
        self.onward(c, 3).wait()
        self.onward(c, 4).wait()


def gather_kernel(n, master_ref, out_ref, own_s, sends, recvs, own_sem):
    at = Peers(n)
    spread = Spread(at, own_s, out_ref, CHUNKS, sends, recvs, own_sem)
    at.greet([at.core_peer, at.y_peer, at.x_peer])
    for c in range(CHUNKS):
        first, last = c * spread.chunk, (c + 1) * spread.chunk
        inside = max(min(last, QUARTER) - first, 0)
        if inside:
            own_s[first : first + inside, :] = master_ref[first : first + inside, :].astype(BF16)
        if first + inside < last:
            own_s[first + inside : last, :] = jnp.zeros((last - first - inside, LANES), BF16)
        spread.start(c)
    for c in range(CHUNKS + 1):
        if c < CHUNKS:
            spread.middle(c)
        if c > 0:
            spread.end(c - 1)
    for c in range(CHUNKS):
        spread.finish(c)


def gather_weights(master, padded, n):
    return pl.pallas_call(
        functools.partial(gather_kernel, n),
        in_specs=[pl.BlockSpec(memory_space=pltpu.VMEM)],
        out_shape=jax.ShapeDtypeStruct((4, padded, LANES), BF16),
        out_specs=pl.BlockSpec(memory_space=pl.ANY),
        scratch_shapes=[
            pltpu.VMEM((padded, LANES), BF16),
            pltpu.SemaphoreType.DMA((CHUNKS, 5)),
            pltpu.SemaphoreType.DMA((CHUNKS, 5)),
            pltpu.SemaphoreType.DMA((CHUNKS,)),
        ],
        compiler_params=pltpu.CompilerParams(collective_id=0, has_side_effects=True, vmem_limit_bytes=VMEM),
        name="gather_weights",
    )(master)


def adam(grad_sum, master, moment_one, moment_two, decay):
    first = BETA_ONE * moment_one + (1.0 - BETA_ONE) * grad_sum
    second = BETA_TWO * moment_two + (1.0 - BETA_TWO) * grad_sum * grad_sum
    first_hat = first * (1.0 / (1.0 - BETA_ONE**STEP))
    second_hat = second * (1.0 / (1.0 - BETA_TWO**STEP))
    return first, second, master - RATE * (first_hat / (jnp.sqrt(second_hat) + ADAM_EPS) + decay * master)


def decay_of(first_row, rows):
    row = first_row + lax.broadcasted_iota(jnp.int32, (rows, LANES), 0)
    return jnp.where(row < MAT_ROWS, DECAY, 0.0)


EARLY = 4
TIMES = ((2, 8, 11, 15, 20, 23, 27, 31), (5, 11, 15, 19, 23, 27, 30, 34), (8, 14, 18, 22, 26, 30, 34, 37), (11, 18, 21, 26, 30, 33, 37, 41))
LATER = ((5, 10, 16, 22), (5, 11, 17, 21))
FIRST_VEC = 17
TAIL_ROWS = QUARTER - QKV_ROWS


def timetable(seqs):
    table = {}

    def put(hook, *what):
        table.setdefault(hook, []).append(what)

    for c in range(EARLY):
        put(0, "early", c, "begin")
        for t, hook in zip((0, 1, 2, 3, 4, 5, "middle", "end"), TIMES[c]):
            put(hook, "early", c, t)
            if t == 5:
                put(hook, "early", c, "update")
    put(0, "state", 0, "begin")
    put(6, "state", 0, "middle")
    put(10, "state", 0, "end")
    put(0, "vectors", 0, "begin")
    put(5, "vectors", 0, "middle")
    put(9, "vectors", 0, "end")
    for u in range(PAIRS - 1):
        at = seqs * STEPS * (u + 1)
        put(at, "late", u, "begin")
        for t, later in enumerate(LATER[u]):
            put(at + later, "late", u, t)
    return table


def attn_backward_kernel(n, scale, x_ref, branch_ref, mixed_ref, att_ref, e_ref, q_ref, k_ref, v_ref, xq_ref, xk_ref, rq_ref, rk_ref, it_ref, wp_ref, vec_ref, tail_ref, g_ref, master_ref, m1_ref, m2_ref, gin_ref, sum_out, late_out, vec_first, vec_rest, state_out, w_ref, n_s, dq_s, dk_s, dv_s, va_s, pg_s, sums_s, heads_s, bias_s, pair_s, core_s, y_s, part_s, land_s, lands_s, new_s, late_s, llands_s, lpart_s, lpieces_s, lstate_s, group_a, dp_a, group_b, dp_b, sum_ref, late_ref, state_ref, o_sems, sends, recvs, loads, w_sends, w_recvs, w_own, l_sends, l_recvs, va_sends, va_recvs, vb_sends, vb_recvs, s_sends, s_recvs, t_sends, t_recvs):
    p, s = pl.program_id(0), pl.program_id(1)
    seqs, seq, _ = x_ref.shape
    blocks = seq // 256
    vec = vec_ref[...].astype(F32)
    fold = lambda v: jnp.sum(v.reshape(v.shape[0] // 8, 8, v.shape[1]), axis=0)
    low = low_half(256)
    base = pl.multiple_of(s * seq, seq)
    at_step = p * seqs + s
    at = Peers(n)
    chunk = part_s.shape[1]
    spread = Spread(at, new_s, w_ref, EARLY, w_sends, w_recvs, w_own)
    early = [Reduction(at, lambda j, c=c: g_ref.at[j, pl.ds(c * chunk, chunk)], loads.at[c], pair_s.at[c], core_s.at[c], y_s.at[c], part_s.at[c], land_s.at[c], lands_s.at[c], sum_ref.at[pl.ds(c * chunk, chunk)], sends.at[c], recvs.at[c]) for c in range(EARLY)]

    def update_late(u, grad):
        g = jnp.minimum(at.shard, 2)
        return adam(grad * scale, lstate_s[g, 0, u], lstate_s[g, 1, u], lstate_s[g, 2, u], DECAY)[2]

    late = [Late(at, late_s.at[u], llands_s.at[u], lpart_s.at[u], lpieces_s.at[u], late_ref.at[u], functools.partial(update_late, u), l_sends.at[u], l_recvs.at[u]) for u in range(PAIRS)]
    rest_sum = Total(at, group_a, dp_a, vec_rest, va_sends, va_recvs)
    first_sum = Total(at, group_b, dp_b, vec_first, vb_sends, vb_recvs)
    tails = Share(at, state_ref, t_sends, t_recvs)
    piece_state = lambda g, peer: remote(lstate_s.at[g], lstate_s.at[g], s_sends.at[g - 1], s_recvs.at[g - 1], peer)

    def state(what):
        if what == "begin":
            first, count = MAT_ROWS - 3 * QUARTER, ALL_ROWS - MAT_ROWS
            for i, ref in enumerate((master_ref, m1_ref, m2_ref)):
                state_ref[at.shard, i] = jnp.zeros(state_ref.shape[2:], F32)
                state_ref[at.shard, i, :TAIL_ROWS, :] = ref[TAIL0:QUARTER, :]
                state_ref[at.shard, i, 16 : 16 + count, :] = ref[first : first + count, :]
            tails.start()

            @pl.when(at.shard == 0)
            def _():
                size = lstate_s.shape[3]
                row = jnp.minimum(at.dp * size, D - size)
                for i, ref in enumerate((master_ref, m1_ref, m2_ref)):
                    for g in range(3):
                        for u in range(PAIRS):
                            lstate_s[g, i, u] = ref[pl.ds(9 * row + 3 * g + u, size, stride=9), :]
                piece_state(1, at.core_peer).start()
                piece_state(2, at.y_peer).start()

        elif what == "middle":
            tails.middle()
        else:
            tails.end()
            for g in (1, 2):

                @pl.when(at.shard == g)
                def _():
                    piece_state(g, at.core_peer).wait_recv()

    def update_early(c):
        first, last = c * chunk, (c + 1) * chunk
        inside = max(min(last, QUARTER) - first, 0)
        if inside:
            rows = slice(first, first + inside)
            grad = sum_ref[rows, :].astype(F32) * scale
            new_s[rows, :] = adam(grad, master_ref[rows, :], m1_ref[rows, :], m2_ref[rows, :], decay_of(at.shard * QUARTER + first, inside))[2].astype(BF16)
        if first + inside < last:
            new_s[first + inside : last, :] = jnp.zeros((last - first - inside, LANES), BF16)

    def act(kind, u, what):
        if kind == "state":
            state(what)
        elif kind == "vectors":
            if what == "begin":
                group_a[at.shard, :TAIL_ROWS, :] = tail_ref[:TAIL_ROWS, :]
                others = ALL_ROWS - MAT_ROWS - FIRST_VEC
                group_a[at.shard, TAIL_ROWS : TAIL_ROWS + others, :] = tail_ref[16 + VEC_AT + FIRST_VEC : 16 + VEC_AT + FIRST_VEC + others, :]
                group_a[at.shard, TAIL_ROWS + others :, :] = jnp.zeros((group_a.shape[1] - TAIL_ROWS - others, LANES), F32)
                rest_sum.begin()
            elif what == "middle":
                rest_sum.middle()
            else:
                rest_sum.end()
        elif kind == "late":
            if what == "begin":
                late[u].begin()
            else:
                late[u].stage(what)
        elif what == "begin":
            early[u].begin()
        elif what == "update":
            update_early(u)
            spread.start(u)
        elif what == "middle":
            spread.middle(u)
        elif what == "end":
            spread.end(u)
        else:
            early[u].stage(what)

    table = timetable(seqs)
    steps = PAIRS * seqs * STEPS

    def hook(k):
        for step in range(PAIRS * seqs):
            actions = table.get(step * STEPS + k)
            if actions:

                @pl.when(at_step == step)
                def _():
                    for action in actions:
                        act(*action)

    @pl.when(at_step == 0)
    def _():
        at.greet([at.group_peer(k) for k in (1, 2, 3)] + [at.dp_peer(k) for k in range(1, n)])
        late_s[...] = jnp.zeros_like(late_s)

    hook(0)

    @pl.when((s == 0) & (p == 0))
    def _():
        heads_s[...] = jnp.zeros_like(heads_s)
        bias_s[...] = jnp.zeros_like(bias_s)
        gain, bias = row_of(vec, NORM_GAIN, 3), row_of(vec, NORM_BIAS, 3)

        def body(i, carry):
            rows = pl.ds(pl.multiple_of(i * 256, 256), 256)
            xhat, _ = norm_stats(x_ref[i // blocks, pl.ds(pl.multiple_of(lax.rem(i, blocks) * 256, 256), 256), :].astype(F32))
            n_s[rows, :] = (xhat * gain + bias).astype(BF16)
            return carry

        lax.fori_loop(0, seqs * blocks, body, 0, unroll=2)

    ones = jnp.ones((256, LANES), F32)
    for i in range(blocks):
        rows = slice(256 * i, 256 * (i + 1))
        v = v_ref[0, 0, rows, :].astype(F32)
        va_s[0, rows, :] = jnp.where(low, v, ones).astype(BF16)
        va_s[1, rows, :] = jnp.where(low, ones, v).astype(BF16)
    swapped = group_matrix(1.0, swapped=True)
    lane = lax.rem(lax.broadcasted_iota(jnp.int32, (256, LANES), 1), HD)
    done = 0
    for i in range(blocks):
        if i:
            hook(i)
        start, width = window(i, blocks)
        first_col = columns(i, blocks)
        rows = slice(256 * i, 256 * (i + 1))
        keys = slice(start, start + width)
        do = (mixed_ref[0, rows, :].astype(F32) * it_ref[0, 0, rows, :]).astype(BF16).astype(F32)
        inner = dot(split(do * att_ref[0, rows, :].astype(F32)), swapped)
        high = inner.astype(BF16).astype(F32)
        extra = jnp.where(lane == 0, -high, jnp.where(lane == 1, high - inner, 0.0))
        q = q_ref[0, 0, rows, :].astype(F32)
        zero = jnp.zeros_like(q)
        dqs, dk, dv = [], None, None
        for h in range(2):
            mine = (lambda a, b: jnp.where(low, a, b).astype(BF16)) if h == 0 else (lambda a, b: jnp.where(low, b, a).astype(BF16))
            e = e_ref[0, 0, 256 * h : 256 * (h + 1), first_col : first_col + width]
            de = dot_nt(mine(do, extra), va_s[h, keys, :])
            ds = e * de.astype(BF16)
            dqs.append(dot(ds, k_ref[0, 0, keys, :]))
            dk_h = dot_tn(ds, mine(q, zero))
            dv_h = dot_tn(e, mine(do, zero))
            dk, dv = (dk_h, dv_h) if h == 0 else (dk + dk_h, dv + dv_h)
        dq_s[rows, :] = jnp.where(low, dqs[0], dqs[1]) * HD**-0.5
        seen = done - start
        if seen > 0:
            dk_s[start:done, :] += dk[:seen]
            dv_s[start:done, :] += dv[:seen]
        if seen < width:
            dk_s[done : start + width, :] = dk[seen:]
            dv_s[done : start + width, :] = dv[seen:]
        done = max(done, start + width)

    hook(blocks)
    qrow, krow = row_of(vec, QUERY, 1), row_of(vec, KEY, 1)
    qg, kg = both_halves(qrow, 0), both_halves(krow, 0)
    means = group_matrix(1.0 / HD)

    def back(d, xhat, r, g):
        e_hat = d * g
        return (e_hat - dot(split(e_hat), means) - xhat * dot(split(e_hat * xhat), means)) * r

    sums = [jnp.zeros((8, LANES), F32)] * 4
    biases = jnp.zeros((8, D), F32)
    for i in range(blocks):
        rows = slice(256 * i, 256 * (i + 1))
        dq, dk, dv = dq_s[rows, :], dk_s[rows, :], dv_s[rows, :]
        xq, xk = xq_ref[0, 0, rows, :].astype(F32), xk_ref[0, 0, rows, :].astype(F32)
        sums = [a + fold(b) for a, b in zip(sums, (dq * xq, dq, dk * xk, dk))]
        pg = jnp.concatenate([back(dq, xq, rq_ref[0, 0, rows, :], qg), back(dk, xk, rk_ref[0, 0, rows, :], kg), dv], axis=1).astype(BF16)
        pg_s[pl.ds(base + 256 * i, 256), pl.ds(pl.multiple_of(p * D, D), D)] = pg
        biases = biases + fold(pg.astype(F32))
    for j in range(4):
        heads_s[j] += sums[j]
    bias_s[p] += biases

    @pl.when(s == seqs - 1)
    def _():
        product = dot_tn(n_s[...], pg_s[:, pl.ds(pl.multiple_of(p * D, D), D)]).astype(BF16)
        for g in range(3):
            late_s[p, g, :D, :] = product[:, g * LANES : (g + 1) * LANES]

    @pl.when((s == seqs - 1) & (p == PAIRS - 1))
    def _():
        gain = row_of(vec, NORM_GAIN, 3)
        late[-1].begin()
        left = [(hook, action) for hook in sorted(table) if hook >= steps for action in table[hook]]

        def due(until):
            while left and left[0][0] < until:
                act(*left.pop(0)[1])

        sums = [jnp.zeros((8, D), F32)] * 2
        for i in range(seqs * blocks):
            rows = slice(i * 256, (i + 1) * 256)
            where, here = i // blocks, slice(i % blocks * 256, (i % blocks + 1) * 256)
            xhat, r = norm_stats(x_ref[where, here, :].astype(F32))
            d = dot_nt(pg_s[rows, :], wp_ref[...])
            e_hat = d * gain
            back = (e_hat - jnp.mean(e_hat, axis=1, keepdims=True) - xhat * jnp.mean(e_hat * xhat, axis=1, keepdims=True)) * r
            gin_ref[where, here, :] = (branch_ref[where, here, :].astype(F32) + back).astype(BF16)
            sums = [sums[0] + fold(d * xhat), sums[1] + fold(d)]
            if i == 3:
                due(steps + 1)
        due(steps + 2)
        sums_s[0], sums_s[1] = sums
        sums = jnp.sum(sums_s[...], axis=1)
        heads = jnp.sum(heads_s[...], axis=1)
        heads = heads + pltpu.roll(heads, HD, 1)
        biases = jnp.sum(bias_s[...], axis=1)

        def put(row, value):
            group_b[at.shard, row : row + 1, :] = value

        for j in range(3):
            part = slice(j * LANES, (j + 1) * LANES)
            put(NORM_GAIN + j, sums[0:1, part])
            put(NORM_BIAS + j, sums[1:2, part])
            for g in range(3):
                put(QKV_BIAS + 3 * g + j, biases[j : j + 1, g * LANES : (g + 1) * LANES])
        put(QUERY, jnp.where(low_half(), heads[0:1], heads[1:2]))
        put(KEY, jnp.where(low_half(), heads[2:3], heads[3:4]))
        group_b[at.shard, FIRST_VEC:, :] = jnp.zeros((group_b.shape[1] - FIRST_VEC, LANES), F32)
        first_sum.begin()
        late[-1].stage(0)
        due(steps + 4)
        first_sum.middle()
        late[-1].stage(1)
        due(steps + 7)
        first_sum.end()
        late[-1].stage(2)
        due(max(table) + 1)
        outs = [pltpu.make_async_copy(state_ref, state_out, o_sems.at[PAIRS]), pltpu.make_async_copy(sum_ref, sum_out, o_sems.at[PAIRS + 1])]
        outs += [pltpu.make_async_copy(late_ref.at[u], late_out.at[u], o_sems.at[u]) for u in range(PAIRS)]
        for out in outs[:-1]:
            out.start()
        late[-1].stage(3)
        outs[-1].start()
        for out in outs:
            out.wait()
        for c in range(EARLY):
            early[c].finish()
            spread.finish(c)
        for u in range(PAIRS):
            late[u].finish()
        rest_sum.finish()
        first_sum.finish()
        tails.finish()

        @pl.when(at.shard == 0)
        def _():
            piece_state(1, at.core_peer).wait_send()
            piece_state(2, at.y_peer).wait_send()


def attn_backward(x, branch, mixed, att, e, q, k, v, xq, xk, rq, rk, it, wp, vec, tail, grads, master, moment_one, moment_two, n, sequences):
    seqs, seq, _ = x.shape
    total = e.shape[-1]
    padded = grads.shape[1]
    chunk = padded // EARLY
    small = whole_rows(D, n, 1)
    piece, lines = small // n, n // 2
    kinds, lates, totals = 3 + 2 * lines, 6 + 2 * n, 2 + n
    rest = TAIL_ROWS + ALL_ROWS - MAT_ROWS - FIRST_VEC
    rest, first = -(-rest // 8) * 8, -(-FIRST_VEC // 8) * 8
    pair = pl.BlockSpec((1, 1, seq, LANES), lambda p, s: (s, p, 0, 0))
    strip = pl.BlockSpec((1, seq, LANES), lambda p, s: (s, 0, p))
    whole = lambda *shape: pl.BlockSpec(shape, lambda p, s: (0,) * len(shape), pipeline_mode=pl.Buffered(1))
    anywhere, vmem = pl.BlockSpec(memory_space=pl.ANY), pl.BlockSpec(memory_space=pltpu.VMEM)
    dma = lambda *shape: pltpu.SemaphoreType.DMA(shape)
    state = whole(QUARTER, LANES)
    return pl.pallas_call(
        functools.partial(attn_backward_kernel, n, 1.0 / sequences),
        grid=(PAIRS, seqs),
        in_specs=[whole(*x.shape), whole(*x.shape), strip, strip, pl.BlockSpec((1, 1, 512, total), lambda p, s: (s, p, 0, 0))]
        + [pair] * 8
        + [whole(*wp.shape), whole(*vec.shape), whole(80, LANES), anywhere, state, state, state],
        out_shape=[
            jax.ShapeDtypeStruct(x.shape, BF16),
            jax.ShapeDtypeStruct((padded, LANES), BF16),
            jax.ShapeDtypeStruct((PAIRS, 2, 4, small, LANES), BF16),
            jax.ShapeDtypeStruct((first, LANES), F32),
            jax.ShapeDtypeStruct((rest, LANES), F32),
            jax.ShapeDtypeStruct((4, 3, 64, LANES), F32),
            jax.ShapeDtypeStruct((4, padded, LANES), BF16),
        ],
        out_specs=[whole(*x.shape), anywhere, anywhere, vmem, vmem, anywhere, anywhere],
        scratch_shapes=[
            pltpu.VMEM((seqs * seq, D), BF16),
            pltpu.VMEM((seq, LANES), F32),
            pltpu.VMEM((seq, LANES), F32),
            pltpu.VMEM((seq, LANES), F32),
            pltpu.VMEM((2, seq, LANES), BF16),
            pltpu.VMEM((seqs * seq, 3 * D), BF16),
            pltpu.VMEM((2, 8, D), F32),
            pltpu.VMEM((4, 8, LANES), F32),
            pltpu.VMEM((PAIRS, 8, D), F32),
            pltpu.VMEM((EARLY, 2, chunk, LANES), BF16),
            pltpu.VMEM((EARLY, 2, chunk, LANES), BF16),
            pltpu.VMEM((EARLY, chunk, LANES), BF16),
            pltpu.VMEM((EARLY, chunk, LANES), BF16),
            pltpu.VMEM((EARLY, chunk // 2, LANES), BF16),
            pltpu.VMEM((EARLY, lines, chunk // 2 // lines, LANES), BF16),
            pltpu.VMEM((padded, LANES), BF16),
            pltpu.VMEM((PAIRS, 4, small, LANES), BF16),
            pltpu.VMEM((PAIRS, 3, small, LANES), BF16),
            pltpu.VMEM((PAIRS, small, LANES), BF16),
            pltpu.VMEM((PAIRS, n, piece, LANES), BF16),
            pltpu.VMEM((3, 3, PAIRS, piece, LANES), F32),
            pltpu.VMEM((4, rest, LANES), F32),
            pltpu.VMEM((n, rest, LANES), F32),
            pltpu.VMEM((4, first, LANES), F32),
            pltpu.VMEM((n, first, LANES), F32),
            pltpu.VMEM((padded, LANES), BF16),
            pltpu.VMEM((PAIRS, 2, 4, small, LANES), BF16),
            pltpu.VMEM((4, 3, 64, LANES), F32),
            dma(PAIRS + 2),
            dma(EARLY, kinds),
            dma(EARLY, kinds),
            dma(EARLY, 2),
            dma(EARLY, 5),
            dma(EARLY, 5),
            dma(EARLY),
            dma(PAIRS, lates),
            dma(PAIRS, lates),
            dma(totals),
            dma(totals),
            dma(totals),
            dma(totals),
            dma(2),
            dma(2),
            dma(3),
            dma(3),
        ],
        compiler_params=pltpu.CompilerParams(collective_id=1, has_side_effects=True, vmem_limit_bytes=62 * 2**20),
        name="attn_backward",
    )(x, branch, mixed, att, e, q, k, v, xq, xk, rq, rk, it, wp, vec, tail, grads, master, moment_one, moment_two)


def finish_kernel(scale, sum_ref, late_ref, first_ref, rest_ref, state_ref, master_ref, m1_ref, m2_ref, w_ref, grad_ref, new_ref, one_ref, two_ref, copy_ref, vec_out, grad_s, flat_s):
    shard = lax.axis_index("shard")
    count = ALL_ROWS - MAT_ROWS
    tail = rest_ref[:TAIL_ROWS, :] * scale
    vec_out[:FIRST_VEC, :] = first_ref[:FIRST_VEC, :] * scale
    vec_out[FIRST_VEC:, :] = rest_ref[TAIL_ROWS : TAIL_ROWS + count - FIRST_VEC, :] * scale

    @pl.when(shard == 0)
    def _():
        for u in range(PAIRS):
            for g in range(3):
                grad_s[pl.ds(3 * g + u, D, stride=9), :] = late_ref[u, 0, g, :D, :].astype(F32) * scale
        grad_s[TAIL0:QUARTER, :] = tail

    @pl.when(shard != 0)
    def _():
        grad_s[...] = sum_ref[:KEPT, :].astype(F32) * scale

    @pl.when(shard == 3)
    def _():
        grad_s[QUARTER - count : QUARTER, :] = vec_out[...]

    grad = grad_s[:QUARTER, :]
    one, two, new = adam(grad, master_ref[...], m1_ref[...], m2_ref[...], decay_of(shard * QUARTER, QUARTER))
    grad_ref[...], one_ref[...], two_ref[...], new_ref[...] = grad, one, two, new
    for u in range(PAIRS):
        for g in range(3):
            flat_s[pl.ds(3 * g + u, D, stride=9), :] = late_ref[u, 1, g, :D, :].astype(F32)
    flat_s[TAIL0:QUARTER, :] = adam(tail, *[state_ref[0, i, :TAIL_ROWS, :] for i in range(3)], DECAY)[2]
    for k in range(1, 4):
        flat_s[k * QUARTER : k * QUARTER + KEPT, :] = w_ref[k - 1, :KEPT, :].astype(F32)
    flat_s[MAT_ROWS:ALL_ROWS, :] = adam(vec_out[...], *[state_ref[3, i, 16 : 16 + count, :] for i in range(3)], 0.0)[2]
    copy_ref[...] = flat_s[:ALL_ROWS, :].astype(BF16)


def finish(sums, late, first, rest, state, master, moment_one, moment_two, weights, sequences):
    f32 = jax.ShapeDtypeStruct((QUARTER, LANES), F32)
    vmem = pl.BlockSpec(memory_space=pltpu.VMEM)
    padded = weights.shape[1]
    return pl.pallas_call(
        functools.partial(finish_kernel, 1.0 / sequences),
        grid=(1,),
        in_specs=[vmem] * 8 + [pl.BlockSpec((pl.Element(3), pl.Element(padded), pl.Element(LANES)), lambda i: (1, 0, 0))],
        out_shape=[f32, f32, f32, f32, jax.ShapeDtypeStruct((ALL_ROWS, LANES), BF16), jax.ShapeDtypeStruct((ALL_ROWS - MAT_ROWS, LANES), F32)],
        out_specs=[vmem] * 6,
        scratch_shapes=[pltpu.VMEM((KEPT, LANES), F32), pltpu.VMEM((3 * QUARTER + KEPT, LANES), F32)],
        compiler_params=pltpu.CompilerParams(vmem_limit_bytes=VMEM),
        name="finish",
    )(sums, late, first, rest, state, master, moment_one, moment_two, weights)


def shards(patches, segments, out_grad, master, moment_one, moment_two):
    seqs, seq, _ = patches.shape
    n = lax.axis_size("dp")
    sequences = seqs * n * lax.axis_size("shard")
    rows = lambda a: a.reshape(QUARTER, LANES)
    master, moment_one, moment_two = rows(master), rows(moment_one), rows(moment_two)
    weights = gather_weights(master, whole_rows(QUARTER, n, CHUNKS), n)
    vec = weights[3, TAIL3:KEPT]
    att, e, q, k, v, xq, xk, rq, rk, it, wp = attn_forward(patches, segments, weights, vec)
    flat = lambda a: a.reshape(seqs * seq, D)
    act, mixed, branch, grads, tail = mlp(flat(patches), flat(att), flat(out_grad), weights, vec)
    whole = lambda a: a.reshape(seqs, seq, D)
    input_grad, sums, late, first, rest, state, weights = attn_backward(
        patches, whole(branch), whole(mixed), att, e, q, k, v, xq, xk, rq, rk, it, wp, vec, tail, grads, master, moment_one, moment_two, n, sequences
    )
    updated = finish(sums, late, first, rest, state, master, moment_one, moment_two, weights, sequences)
    grad_sum, new_master, first_moment, second_moment, weights_copy, vector_grad = [a.reshape(-1) for a in updated]
    return whole(act), input_grad, grad_sum, vector_grad, new_master, first_moment, second_moment, weights_copy


def solution(mesh):
    split_rows = P(("dp", "shard"), None, None)
    return jax.shard_map(
        shards,
        mesh=mesh,
        in_specs=(split_rows, P(("dp", "shard"), None), split_rows, P("shard"), P("shard"), P("shard")),
        out_specs=(split_rows, split_rows, P("shard"), P(), P("shard"), P("shard"), P("shard"), P()),
        check_vma=False,
    )
```
